512 devices in a mesh: ctx: 16 (over z_lo, core), exp: 32 (over z_hi, x, y).
Axes of the slice: x: 4, y: 4, z: 16 (z_hi: 2, z_lo: 8; z = z_hi * 8 + z_lo), core: 2. Of those that a mesh axis runs over, the one named last changes fastest.
Arguments:
- query: bfloat16 [32, 2048, 4096], P('exp', 'ctx'), may hold values from -41 to 41
- keyval: bfloat16 [32, 2, 2048, 256], P('exp', None, 'ctx'), may hold values from -4 to 4
- doc_ids: int32 [32, 2048], P('exp', 'ctx'), may hold values from 0 to 5, never falling along the last dimension, each value on 1 to 1024 neighbouring positions
- route_ids: int32 [32, 2048], P('exp', 'ctx'), may hold values from 0 to 63
- combine: float32 [32, 2048], P('exp', 'ctx'), may hold values from 0.5 to 2
- w_gate_up: bfloat16 [32, 2, 1536, 4096], P('exp', None, 'ctx'), may hold values from -0.09375 to 0.09375
- w_down: bfloat16 [32, 1536, 4096], P('exp', None, 'ctx'), may hold values from -0.15625 to 0.15625
Outputs:
- layer_out: bfloat16 [32, 2048, 4096], P('exp', 'ctx')
The draws below stay inside these ranges and needn't reach their ends.
All inputs are finite; a program needn't handle non-finite values.
Results may differ from the reference program's by a relative error of at most 0.024.
Values may be sent and summed in bfloat16 or wider, within the bound.
A program may use at most 128 MiB of HBM per device.

```python
import math
import jax
import jax.numpy as jnp
import numpy as np
from jax import lax

D = 4096
FF = 1536
HD = 128
QH = 32
KVH = 2
CAP = 2
DOCS = 6
TOK_DEV = 128
LEN = 2048
SEQS = 32
EXPERTS = 32
N_CTX = 16


def joint_draw(key):
    key_query = jax.random.fold_in(key, 11)
    key_keys = jax.random.fold_in(key, 12)
    key_values = jax.random.fold_in(key, 13)
    head_group = QH // KVH
    queries = jax.random.truncated_normal(key_query, -4.0, 4.0, (SEQS, LEN, KVH, head_group, HD), jnp.float32)
    key_rows = jax.random.truncated_normal(key_keys, -4.0, 4.0, (SEQS, LEN, KVH, HD), jnp.float32)
    value_rows = jax.random.truncated_normal(key_values, -4.0, 4.0, (SEQS, LEN, KVH, HD), jnp.float32)
    query_out = queries.reshape(SEQS, LEN, QH * HD).astype(jnp.bfloat16)
    keyval_out = jnp.stack([key_rows.reshape(SEQS, LEN, KVH * HD), value_rows.reshape(SEQS, LEN, KVH * HD)], axis=1).astype(jnp.bfloat16)
    return (query_out, keyval_out)


def draw_query(key, part):
    return joint_draw(key)[0]


def draw_keyval(key, part):
    return joint_draw(key)[1]


def set_ends(values, stream_key, low, largest):
    longest = values.shape.index(max(values.shape))
    spots = []
    for shift in (0, 1):
        where = [jax.random.randint(jax.random.fold_in(stream_key, axis), (), 0, length) for axis, length in enumerate(values.shape)]
        where[longest] = (where[longest] + shift) % values.shape[longest]
        spots.append(tuple(where))
    return values.at[spots[0]].set(low).at[spots[1]].set(largest)


def block_levels(rng, extent, shards, least, high):
    def one(axis_at, parts):
        steps = jax.random.uniform(jax.random.fold_in(jax.random.fold_in(rng, 6), axis_at), (parts,), jnp.float32, least / len(shards), high / len(shards))
        return jnp.repeat(jnp.exp(steps), extent[axis_at] // parts).reshape((-1,) + (1,) * (len(extent) - axis_at - 1))

    loudness = one(*shards[0])
    for cut in shards[1:]:
        loudness = loudness * one(*cut)
    return loudness


def length_profile(count, total, reach, lean):
    loads = [(1 << 20) // math.isqrt(rank ** lean) + 1 for rank in range(2, count + 1)]
    rest, holding = total - reach - (count - 1), [1] * (count - 1)
    while rest > 0:
        free = [i for i in range(count - 1) if holding[i] < reach]
        mass, remaining = sum([loads[i] for i in free]), rest
        for i in free:
            extra = min(reach - holding[i], max(1, remaining * loads[i] // mass), rest)
            holding[i] = holding[i] + extra
            rest = rest - extra
    return np.array([reach] + holding)


def ragged_sizes(stream_key, number_of, total, limit, lean):
    if number_of == 2:
        one = jax.random.randint(stream_key, (), max(1, total - limit), min(limit, total - 1) + 1)
        return jnp.stack([one, total - one])
    tallies = jnp.asarray(length_profile(number_of, total, limit, lean), jnp.int32)
    pairs = (number_of - 1) // 2
    giver, taker = tallies[1:1 + 2 * pairs:2], tallies[2:2 + 2 * pairs:2]
    margin = jnp.minimum(giver - 1, limit - taker)
    passed = jax.random.randint(jax.random.fold_in(stream_key, 1), (pairs,), 0, 1 << 20) % (margin + 1)
    tallies = tallies.at[1:1 + 2 * pairs:2].set(giver - passed).at[2:2 + 2 * pairs:2].set(taker + passed)
    return tallies[jax.random.permutation(jax.random.fold_in(stream_key, 2), number_of)]


def bell_draw(rng, dims, width, limit, cuts=(), kind=jnp.bfloat16):
    entries = jax.random.normal(rng, dims, jnp.float32) * width
    if len(cuts) > 0:
        entries = block_levels(rng, dims, cuts, -0.22, 0.18) * entries
    return jnp.clip(entries, min=-limit, max=limit).astype(kind)


def setup_inputs(seed: int = 0) -> dict:
    key_list = jax.random.split(jax.random.key(seed), 8)
    query = draw_query(jax.random.fold_in(key_list[7], 71), 0)
    keyval = draw_keyval(jax.random.fold_in(key_list[7], 71), 0)
    doc_ids = jax.vmap(lambda own: jnp.searchsorted(jnp.cumsum(ragged_sizes(own, DOCS, LEN, LEN // 2, 0)), jnp.arange(LEN), side="right"))(jax.random.split(key_list[2], SEQS)).reshape((SEQS, LEN)).astype(jnp.int32)
    route_ids = set_ends(jax.random.randint(key_list[3], (SEQS, LEN), 0, 2 * EXPERTS), jax.random.fold_in(key_list[3], 1), 0, (2 * EXPERTS) - 1).astype(jnp.int32)
    combine = jnp.clip(jnp.exp(math.log(2.0) - 1.3862944 * jax.random.uniform(key_list[4], (SEQS, LEN), jnp.float32) ** block_levels(key_list[4], (SEQS, LEN), ((0, 32), (1, 16)), -0.2, 0.2)), 0.5, 2.0)
    w_gate_up = bell_draw(key_list[5], (EXPERTS, 2, FF, D), D ** -0.5, 0.09375, ((0, 32), (2, 16)))
    w_down = bell_draw(key_list[6], (EXPERTS, FF, D), FF ** -0.5, 0.15625, ((0, 32), (2, 16)))
    return {"query": query, "keyval": keyval, "doc_ids": doc_ids, "route_ids": route_ids, "combine": combine, "w_gate_up": w_gate_up, "w_down": w_down}


neg_large = -1e+30
norm_eps = 1e-06

def head_output(q_one, k_one, v_one, doc_row):
    scores = jnp.dot(q_one, k_one.T, preferred_element_type=jnp.float32) * HD ** (-0.5)
    allowed = doc_row[None, :] == doc_row[:, None]
    masked = jnp.where(allowed, scores, neg_large)
    row_max = lax.optimization_barrier(jnp.max(masked, axis=1, keepdims=True))
    weights = jnp.where(allowed, jnp.exp(masked - row_max), 0.0)
    denominator = lax.optimization_barrier(jnp.sum(weights, axis=1, keepdims=True))
    mixed = jnp.dot(weights.astype(jnp.bfloat16), v_one, preferred_element_type=jnp.float32)
    return mixed / denominator

def sequence_attention(operands):
    q_seq, kv_seq, doc_row = operands
    head_group = QH // KVH
    q_heads = q_seq.reshape(LEN, QH, HD).transpose(1, 0, 2)
    k_heads = jnp.repeat(kv_seq[0].reshape(LEN, KVH, HD).transpose(1, 0, 2), head_group, axis=0)
    v_heads = jnp.repeat(kv_seq[1].reshape(LEN, KVH, HD).transpose(1, 0, 2), head_group, axis=0)

    def one_head(triple):
        q_one, k_one, v_one = triple
        return head_output(q_one, k_one, v_one, doc_row)
    outputs = lax.map(one_head, (q_heads, k_heads, v_heads))
    return outputs.transpose(1, 0, 2).reshape(LEN, QH * HD).astype(jnp.bfloat16)

def expert_rows(operands):
    rows, gate_up, down = operands
    gate = jnp.dot(rows, gate_up[0].T, preferred_element_type=jnp.float32)
    upper = jnp.dot(rows, gate_up[1].T, preferred_element_type=jnp.float32)
    hidden = (jax.nn.silu(gate) * upper).astype(jnp.bfloat16)
    return jnp.dot(hidden, down, preferred_element_type=jnp.float32).astype(jnp.bfloat16)

def reference(query, keyval, doc_ids, route_ids, combine, w_gate_up, w_down):
    attended = lax.map(sequence_attention, (query, keyval, doc_ids))
    flat = attended.astype(jnp.float32)
    normed = (flat * lax.rsqrt(lax.optimization_barrier(jnp.mean(flat * flat, axis=-1, keepdims=True)) + norm_eps)).astype(jnp.bfloat16)
    ids = route_ids.reshape(SEQS, N_CTX, TOK_DEV)
    expert_ids = jnp.arange(EXPERTS, dtype=jnp.int32)
    onehot = (ids[..., None] == expert_ids).astype(jnp.int32)
    earlier = lax.optimization_barrier(jnp.sum((jnp.cumsum(onehot, axis=2) - onehot) * onehot, axis=-1))
    kept = (ids < EXPERTS) & (earlier < CAP)
    slot = jnp.where(kept, ids * CAP + earlier, -1)
    slot_ids = jnp.arange(EXPERTS * CAP, dtype=jnp.int32)
    blocks = normed.reshape(SEQS, N_CTX, TOK_DEV, D)

    def pack(operands):
        slot_seq, block_seq = operands
        chooser = (slot_seq[:, None, :] == slot_ids[None, :, None]).astype(jnp.float32)
        return jnp.einsum('nct,ntd->ncd', chooser, block_seq.astype(jnp.float32)).astype(jnp.bfloat16)
    packed = lax.map(pack, (slot, blocks))
    grouped = packed.reshape(SEQS * N_CTX, EXPERTS, CAP, D).transpose(1, 0, 2, 3).reshape(EXPERTS, SEQS * N_CTX * CAP, D)
    produced = lax.map(expert_rows, (grouped, w_gate_up, w_down))
    regrouped = produced.reshape(EXPERTS, SEQS, N_CTX, CAP, D).transpose(1, 2, 0, 3, 4).reshape(SEQS, N_CTX, EXPERTS * CAP, D)

    def unpack(operands):
        slot_seq, made = operands
        chooser = (slot_seq[:, None, :] == slot_ids[None, :, None]).astype(jnp.float32)
        return jnp.einsum('nct,ncd->ntd', chooser, made.astype(jnp.float32))
    picked = lax.map(unpack, (slot, regrouped)).reshape(SEQS, LEN, D)
    return (flat + combine[..., None] * picked).astype(jnp.bfloat16)
```

```python
import functools

import jax
import jax.numpy as jnp
from jax import lax
from jax.experimental import pallas as pl
from jax.experimental.pallas import tpu as pltpu
from jax.sharding import PartitionSpec as P

HD = 128
CAP = 2
EPS = 1e-06
LOWEST = -1e30
LOG2E = 1.4426950408889634
REACH = 1024

BF = jnp.bfloat16
F32 = jnp.float32
MESH = pl.DeviceIdType.MESH
NT = (((1,), (1,)), ((), ()))
TN = (((0,), (0,)), ((), ()))


def remote(src, dst, send_sem, recv_sem, target):
    return pltpu.make_async_remote_copy(
        src_ref=src,
        dst_ref=dst,
        send_sem=send_sem,
        recv_sem=recv_sem,
        device_id=target,
        device_id_type=MESH,
    )


def spread_kernel(
    nctx, kv_ref, doc_ref, kv_out, doc_out, got, got_doc, sent, sent_doc, shown, shown_doc
):
    tok = kv_ref.shape[1]
    seg = nctx // 2
    reach = min(seg - 1, -(-REACH // (2 * tok)))
    ctx = lax.axis_index("ctx")
    exp = lax.axis_index("exp")
    core = lax.rem(ctx, 2)
    pos = ctx // 2
    sibling = (ctx + 1 - 2 * core, exp)

    def block(b):
        return pl.ds(pl.multiple_of(b * tok, tok), tok)

    def neighbour(way):
        return (ctx + 2 * way, exp)

    def has(p):
        return jnp.logical_and(p >= 0, p < seg)

    barrier = pltpu.get_barrier_semaphore()
    pl.semaphore_signal(barrier, inc=1, device_id=sibling, device_id_type=MESH)
    for way in (1, -1):

        @pl.when(has(pos + way))
        def _():
            pl.semaphore_signal(barrier, inc=1, device_id=neighbour(way), device_id_type=MESH)

    pl.semaphore_wait(
        barrier, 1 + (pos > 0).astype(jnp.int32) + (pos < seg - 1).astype(jnp.int32)
    )

    def moves(b, sems, doc_sem, target, first):
        out = []
        for part in range(2):
            src = kv_ref.at[part] if first else kv_out.at[part, block(b)]
            out.append(
                remote(src, kv_out.at[part, block(b)], sems.at[part], got.at[b, part], target)
            )
        src = doc_ref if first else doc_out.at[b]
        out.append(remote(src, doc_out.at[b], doc_sem, got_doc.at[b], target))
        return out

    def along(way, t, b):
        d = 0 if way == 1 else 1
        return moves(b, sent.at[d, t], sent_doc.at[d, t], neighbour(way), t == 0)

    def across(b, first):
        return moves(b, shown.at[b], shown_doc.at[b], sibling, first)

    for way in (1, -1):

        @pl.when(has(pos + way))
        def _():
            for copy in along(way, 0, ctx):
                copy.start()

    for copy in across(ctx, True):
        copy.start()
    kv_out[:, block(ctx), :] = kv_ref[...]
    doc_out[ctx] = doc_ref[...]

    for t in range(1, reach + 1):
        for way in (1, -1):
            source = pos - way * t
            b = 2 * source + core

            @pl.when(has(source))
            def _():
                there = across(b, False)
                on = along(way, t, b) if t < reach else None
                for n in range(3):
                    there[n].wait_recv()
                    if on is not None:

                        @pl.when(has(pos + way))
                        def _():
                            on[n].start()

                    there[n].start()

    for t in range(0, reach + 1):
        for way in (1, -1):
            source = pos - way * t
            b = 2 * source + core

            @pl.when(has(source))
            def _():
                if t > 0 or way == 1:
                    for copy in across(2 * source + 1 - core, False):
                        copy.wait_recv()
                    for copy in across(b, False):
                        copy.wait_send()
                if t < reach:

                    @pl.when(has(pos + way))
                    def _():
                        for copy in along(way, t, b):
                            copy.wait_send()


def spread(kv, doc, nctx):
    _, tok, width = kv.shape
    return pl.pallas_call(
        functools.partial(spread_kernel, nctx),
        out_shape=(
            jax.ShapeDtypeStruct((2, nctx * tok, width), BF),
            jax.ShapeDtypeStruct((nctx, 8, tok), jnp.int32),
        ),
        in_specs=[pl.BlockSpec(memory_space=pltpu.VMEM)] * 2,
        out_specs=(pl.BlockSpec(memory_space=pltpu.VMEM),) * 2,
        scratch_shapes=[
            pltpu.SemaphoreType.DMA((nctx, 2)),
            pltpu.SemaphoreType.DMA((nctx,)),
            pltpu.SemaphoreType.DMA((2, 8, 2)),
            pltpu.SemaphoreType.DMA((2, 8)),
            pltpu.SemaphoreType.DMA((nctx, 2)),
            pltpu.SemaphoreType.DMA((nctx,)),
        ],
        compiler_params=pltpu.CompilerParams(
            collective_id=0, has_side_effects=True, vmem_limit_bytes=16 << 20
        ),
    )(kv, doc)


def wanted_slot(r, columns):
    d, i = r // 16, lax.rem(r, 4)
    return (columns * (i // 2) + d) * CAP + lax.rem(i, 2)


def quarter_of(r):
    return lax.rem(r, 16) // 4


def slots(ids, earlier, experts):
    kept = jnp.logical_and(ids < experts, earlier < CAP)
    return jnp.where(kept, ids * CAP + earlier, -1)


def attend_kernel(
    experts, kv_ref, doc_ref, q_ref, qdoc_ref, idr_ref, idc_ref, att_ref, send_ref, s_scr, m_scr, l_scr, a_scr
):
    tok, width = q_ref.shape
    nctx = doc_ref.shape[0]
    groups = kv_ref.shape[2] // HD
    per = width // HD // groups
    step = 2 * tok
    seg = nctx // 2
    reach = min(seg - 1, -(-REACH // step))
    pos = lax.axis_index("ctx") // 2
    scale = HD ** (-0.5) * LOG2E

    where = lax.broadcasted_iota(jnp.int32, (nctx, 8, tok), 0) // 2
    docs = jnp.where(where < pos - reach, -1, jnp.where(where > pos + reach, 1 << 20, doc_ref[...]))
    qdoc = qdoc_ref[...]
    low = jnp.min(qdoc)
    high = jnp.max(qdoc)
    begin = jnp.sum((docs < low).astype(jnp.int32)) // 8
    end = jnp.sum((docs <= high).astype(jnp.int32)) // 8
    first = begin // step
    last = (end + step - 1) // step

    squares = jnp.zeros((tok, HD), F32)
    for g in range(groups):
        lanes = slice(g * HD, (g + 1) * HD)
        m_scr[...] = jnp.full(m_scr.shape, LOWEST, F32)
        l_scr[...] = jnp.zeros(l_scr.shape, F32)
        a_scr[...] = jnp.zeros(a_scr.shape, F32)

        @pl.loop(first, last)
        def _(kb):
            keys = kv_ref[0, pl.ds(pl.multiple_of(kb * step, step), step), lanes]
            kdoc = jnp.concatenate([doc_ref[2 * kb, 0:1], doc_ref[2 * kb + 1, 0:1]], axis=1)
            bias = jnp.where(kdoc == qdoc, 0.0, LOWEST).astype(F32)
            for h in range(per):
                at = slice((g * per + h) * HD, (g * per + h + 1) * HD)
                rows = slice(h * tok, (h + 1) * tok)
                s = lax.dot_general(q_ref[:, at], keys, NT, preferred_element_type=F32) + bias
                s_scr[kb, rows] = s
                m_scr[rows] = jnp.maximum(
                    m_scr[rows], jnp.maximum(s[:, :HD], s[:, HD:])
                )

        for h in range(per):
            rows = slice(h * tok, (h + 1) * tok)
            m_scr[rows] = jnp.broadcast_to(
                jnp.max(m_scr[rows], axis=1, keepdims=True), (tok, HD)
            )

        @pl.loop(first, last)
        def _(kb):
            values = kv_ref[1, pl.ds(pl.multiple_of(kb * step, step), step), lanes]
            for h in range(per):
                rows = slice(h * tok, (h + 1) * tok)
                top = m_scr[rows]
                s = s_scr[kb, rows]
                p = jnp.exp2((s - jnp.concatenate([top, top], axis=1)) * scale)
                l_scr[rows] = l_scr[rows] + (p[:, :HD] + p[:, HD:])
                a_scr[rows] = a_scr[rows] + jnp.dot(
                    p.astype(BF), values, preferred_element_type=F32
                )

        for h in range(per):
            at = slice((g * per + h) * HD, (g * per + h + 1) * HD)
            rows = slice(h * tok, (h + 1) * tok)
            total = jnp.sum(l_scr[rows], axis=1, keepdims=True)
            mixed = (a_scr[rows] / total).astype(BF)
            att_ref[:, at] = mixed
            wide = mixed.astype(F32)
            squares = squares + wide * wide

    inverse = lax.rsqrt(jnp.sum(squares, axis=1, keepdims=True) / width + EPS)
    idr = idr_ref[0:1]
    idc = idc_ref[...]
    before = lax.broadcasted_iota(jnp.int32, (tok, tok), 0) < lax.broadcasted_iota(
        jnp.int32, (tok, tok), 1
    )
    earlier = jnp.sum(
        jnp.where(jnp.logical_and(before, idc == idr), 1, 0), axis=0, keepdims=True
    )
    slot = slots(idr, earlier, experts)
    count = send_ref.shape[0]
    r = lax.broadcasted_iota(jnp.int32, (count, tok), 0)
    match = wanted_slot(r, count // 16) == slot
    part = quarter_of(r)
    span = width // 4
    for piece in range(0, span, 256):
        total = jnp.zeros((count, 256), F32)
        for q in range(4):
            chooser = jnp.where(jnp.logical_and(match, part == q), 1.0, 0.0).astype(BF)
            att = att_ref[:, q * span + piece : q * span + piece + 256].astype(F32)
            normed = (att * inverse).astype(BF)
            total = total + jnp.dot(chooser, normed, preferred_element_type=F32)
        send_ref[:, piece : piece + 256] = total.astype(BF)


def attend(kv, doc, q, qdoc, idr, idc, experts):
    tok, width = q.shape
    nctx = doc.shape[0]
    per = width // HD // (kv.shape[2] // HD)
    count = 16 * (experts // 2)
    vm = pl.BlockSpec(memory_space=pltpu.VMEM)
    return pl.pallas_call(
        functools.partial(attend_kernel, experts),
        out_shape=(
            jax.ShapeDtypeStruct((tok, width), BF),
            jax.ShapeDtypeStruct((count, width // 4), BF),
        ),
        in_specs=[vm] * 6,
        out_specs=(vm, vm),
        scratch_shapes=[
            pltpu.VMEM((nctx // 2, per * tok, 2 * tok), F32),
            pltpu.VMEM((per * tok, HD), F32),
            pltpu.VMEM((per * tok, HD), F32),
            pltpu.VMEM((per * tok, HD), F32),
        ],
        compiler_params=pltpu.CompilerParams(vmem_limit_bytes=48 << 20),
    )(kv, doc, q, qdoc, idr, idc)


def experts_kernel(
    nctx, nexp, send_ref, wgu_ref, wd_ref, back_ref,
    came, rows, transit, hid, made, ret, send2, back,
    a_sent, a_got, r_sent, r_got, t_sent, t_got, x_sent, x_got,
    h_sent, h_got, y_sent, y_got, d_sent, d_got, b_sent, b_got,
):
    seg = nctx // 2
    half = seg // 2
    xy = nexp // 2
    span = send_ref.shape[1]
    width = 4 * span
    piece = xy
    units = wgu_ref.shape[0] // 2
    cols = wd_ref.shape[1]
    ctx = lax.axis_index("ctx")
    exp = lax.axis_index("exp")
    core = lax.rem(ctx, 2)
    pos = ctx // 2
    zhi = exp // xy
    place = lax.rem(exp, xy)
    layer = zhi * seg + pos
    layers = 2 * seg
    sibling = (ctx + 1 - 2 * core, exp)

    def at_layer(z, c):
        z = lax.rem(z + 2 * layers, layers)
        return (2 * lax.rem(z, seg) + c, (z // seg) * xy + place)

    def at_place(d):
        return (ctx, zhi * xy + d)

    barrier = pltpu.get_barrier_semaphore()

    @pl.loop(1, xy)
    def _(j):
        pl.semaphore_signal(
            barrier, inc=1, device_id=at_place(lax.rem(place + j, xy)), device_id_type=MESH
        )

    @pl.loop(1, 2 * layers)
    def _(j):
        me = 2 * layer + core
        n = lax.rem(me + j, 2 * layers)
        pl.semaphore_signal(
            barrier, inc=1, device_id=at_layer(n // 2, lax.rem(n, 2)), device_id_type=MESH
        )

    pl.semaphore_wait(barrier, xy - 1 + 2 * layers - 1)

    def block16(d):
        return pl.ds(pl.multiple_of(d * 16, 16), 16)

    def swap(src, dst, sent, got, d):
        out = remote(src.at[block16(d)], dst.at[block16(place)], sent.at[d], got.at[place], at_place(d))
        into = remote(src.at[block16(place)], dst.at[block16(d)], sent.at[place], got.at[d], at_place(d))
        return out, into

    def exchange(src, dst, sent, got):
        @pl.loop(1, xy)
        def _(j):
            swap(src, dst, sent, got, lax.rem(place + j, xy))[0].start()

        dst[block16(place)] = src[block16(place)]

        @pl.loop(1, xy)
        def _(j):
            swap(src, dst, sent, got, lax.rem(place + xy - j, xy))[1].wait_recv()

    def exchange_end(src, dst, sent, got):
        @pl.loop(1, xy)
        def _(j):
            swap(src, dst, sent, got, lax.rem(place + j, xy))[0].wait_send()

    exchange(send_ref, came, a_sent, a_got)
    r = lax.broadcasted_iota(jnp.int32, (2 * xy, 16 * xy), 0)
    c = lax.broadcasted_iota(jnp.int32, (2 * xy, 16 * xy), 1)
    for side in range(2):
        z = zhi if side == 0 else 1 - zhi
        for q in range(4):
            pick = jnp.where(
                c == (r // 2) * 16 + q * 4 + 2 * z + lax.rem(r, 2), 1.0, 0.0
            ).astype(BF)
            got = jnp.dot(pick, came[...], preferred_element_type=F32).astype(BF)
            for h in range(2):
                kept = got[h * piece : (h + 1) * piece]
                if side == 0:
                    rows[layer, core, h, :, q * span : (q + 1) * span] = kept
                else:
                    transit[pos, h, :, q * span : (q + 1) * span] = kept

    def ring(z):
        return lax.rem(z + 2 * layers, layers)

    def rank_of(way):
        return pos if way == 1 else seg - 1 - pos

    def chunk_moves(way, t, h):
        d = 0 if way == 1 else 1
        k = rank_of(way)
        z = ring(layer - way * (t - 1))
        p = lax.rem(pos - way * (t - 1) + 2 * seg, seg)
        target = at_layer(layer + way, core)
        return [
            (
                jnp.logical_and(k < seg - 1, t <= k + 1 - half),
                remote(transit.at[p, h], transit.at[p, h], t_sent.at[d, t, h], t_got.at[p, h], target),
            ),
            (
                jnp.logical_and(k == seg - 1, t <= half),
                remote(transit.at[p, h], rows.at[z, core, h], t_sent.at[d, t, h], r_got.at[z, h], target),
            ),
            (
                jnp.logical_and(k < seg - 1, t <= k + 1 + half),
                remote(rows.at[z, core, h], rows.at[z, core, h], r_sent.at[d, t, h], r_got.at[z, h], target),
            ),
        ]

    def chunk_start(way, t, h):
        for cond, copy in chunk_moves(way, t, h):

            @pl.when(cond)
            def _():
                copy.start()

    def show(z, h, c):
        return remote(rows.at[z, c, h], rows.at[z, c, h], x_sent.at[z, h], x_got.at[z, h], sibling)

    for h in range(2):
        for way in (1, -1):
            chunk_start(way, 1, h)
        show(layer, h, core).start()

    steps = seg - 1 + half

    @pl.loop(1, steps + 1)
    def _(t):
        for h in range(2):
            for way in (1, -1):
                k = rank_of(way)
                z = ring(layer - way * t)
                p = lax.rem(pos - way * t + 2 * seg, seg)

                @pl.when(t <= k - half)
                def _():
                    remote(
                        transit.at[p, h], transit.at[p, h], t_sent.at[0, 0, h], t_got.at[p, h], sibling
                    ).wait_recv()

                @pl.when(t <= k + half)
                def _():
                    remote(
                        rows.at[z, core, h], rows.at[z, core, h], r_sent.at[0, 0, h], r_got.at[z, h], sibling
                    ).wait_recv()

                chunk_start(way, t + 1, h)

                @pl.when(t <= k + half)
                def _():
                    show(z, h, core).start()

    @pl.loop(0, layers)
    def _(z):
        for h in range(2):
            show(z, h, 1 - core).wait_recv()

    def hid_moves(way, t, s):
        d = 0 if way == 1 else 1
        k = rank_of(way)
        b = 2 * (pos - way * (t - 1)) + core
        target = (ctx + 2 * way, exp)
        return (
            jnp.logical_and(k < seg - 1, t <= k + 1),
            remote(hid.at[s, b], hid.at[s, b], h_sent.at[d, t, s], h_got.at[s, b], target),
        )

    def hid_start(way, t, s):
        cond, copy = hid_moves(way, t, s)

        @pl.when(cond)
        def _():
            copy.start()

    def hid_show(s, b):
        return remote(hid.at[s, b], hid.at[s, b], y_sent.at[s, b], y_got.at[s, b], sibling)

    chunk = 4 * xy
    some = seg * chunk
    for s in range(2):
        x = rows[s * seg : (s + 1) * seg].reshape(some, width)
        both = lax.dot_general(wgu_ref[...], x, NT, preferred_element_type=F32)
        gate, upper = both[:units], both[units:]
        hid[s, ctx] = (gate / (1.0 + jnp.exp(-gate)) * upper).astype(BF)
        for way in (1, -1):
            hid_start(way, 1, s)
        hid_show(s, ctx).start()

    @pl.loop(1, seg)
    def _(t):
        for s in range(2):
            for way in (1, -1):
                k = rank_of(way)
                b = 2 * (pos - way * t) + core

                @pl.when(t <= k)
                def _():
                    remote(
                        hid.at[s, b], hid.at[s, b], h_sent.at[0, 0, s], h_got.at[s, b], sibling
                    ).wait_recv()

                hid_start(way, t + 1, s)

                @pl.when(t <= k)
                def _():
                    hid_show(s, b).start()

    fold = nctx // 4

    def home(z, c):
        slot = (lax.rem(ctx, fold), zhi, ctx // fold)
        n = zhi * nctx + ctx
        return remote(
            made.at[z, c], ret.at[slot], d_sent.at[2 * z + c], d_got.at[n], at_layer(z, c)
        )

    def home_from(z, c):
        n_ctx = 2 * lax.rem(z, seg) + c
        n = (z // seg) * nctx + n_ctx
        slot = (lax.rem(n_ctx, fold), z // seg, n_ctx // fold)
        return remote(made.at[z, c], ret.at[slot], d_sent.at[2 * z + c], d_got.at[n], at_layer(z, c))

    for s in range(2):

        @pl.loop(0, seg)
        def _(p):
            hid_show(s, 2 * p + 1 - core).wait_recv()

        hidden = hid[s].reshape(nctx * units, some)
        out = lax.dot_general(hidden, wd_ref[...], TN, preferred_element_type=F32)
        made[s * seg : (s + 1) * seg] = out.astype(BF).reshape(seg, 2, 2 * xy, cols)

        me = 2 * layer + core

        @pl.loop(0, nctx)
        def _(j):
            n = lax.rem(me + j, nctx) + s * nctx

            @pl.when(n != me)
            def _():
                home(n // 2, lax.rem(n, 2)).start()

    ret[lax.rem(ctx, fold), zhi, ctx // fold] = made[layer, core]

    @pl.loop(1, 2 * layers)
    def _(j):
        n = lax.rem(2 * layer + core + j, 2 * layers)
        home_from(n // 2, lax.rem(n, 2)).wait_recv()

    r = lax.broadcasted_iota(jnp.int32, (16 * xy, 16 * xy), 0)
    c = lax.broadcasted_iota(jnp.int32, (16 * xy, 16 * xy), 1)
    i = lax.rem(r, 4)
    place_back = jnp.where(
        c == ((i // 2) * 4 + quarter_of(r)) * 2 * xy + 2 * (r // 16) + lax.rem(i, 2), 1.0, 0.0
    ).astype(BF)
    for m in range(fold):
        got = ret[m].reshape(16 * xy, cols)
        send2[:, m * cols : (m + 1) * cols] = jnp.dot(
            place_back, got, preferred_element_type=F32
        ).astype(BF)
    exchange(send2, back, b_sent, b_got)
    back_ref[...] = back[...]

    exchange_end(send_ref, came, a_sent, a_got)
    exchange_end(send2, back, b_sent, b_got)

    @pl.loop(1, steps + 2)
    def _(t):
        for h in range(2):
            for way in (1, -1):
                for cond, copy in chunk_moves(way, t, h):

                    @pl.when(cond)
                    def _():
                        copy.wait_send()

    @pl.loop(0, layers)
    def _(z):
        for h in range(2):
            show(z, h, core).wait_send()

    @pl.loop(1, seg + 1)
    def _(t):
        for s in range(2):
            for way in (1, -1):
                cond, copy = hid_moves(way, t, s)

                @pl.when(cond)
                def _():
                    copy.wait_send()

    @pl.loop(0, seg)
    def _(p):
        for s in range(2):
            hid_show(s, 2 * p + core).wait_send()

    @pl.loop(1, 2 * layers)
    def _(j):
        n = lax.rem(2 * layer + core + j, 2 * layers)
        home(n // 2, lax.rem(n, 2)).wait_send()


def run_experts(send, wgu, wd, nctx, nexp):
    xy = nexp // 2
    seg = nctx // 2
    layers = 2 * seg
    span = send.shape[1]
    width = 4 * span
    units = wgu.shape[0] // 2
    cols = wd.shape[1]
    dma = pltpu.SemaphoreType.DMA
    vm = pl.BlockSpec(memory_space=pltpu.VMEM)
    return pl.pallas_call(
        functools.partial(experts_kernel, nctx, nexp),
        out_shape=jax.ShapeDtypeStruct(send.shape, BF),
        in_specs=[vm] * 3,
        out_specs=vm,
        scratch_shapes=[
            pltpu.VMEM(send.shape, BF),
            pltpu.VMEM((layers, 2, 2, xy, width), BF),
            pltpu.VMEM((seg, 2, xy, width), BF),
            pltpu.VMEM((2, nctx, units, seg * 4 * xy), BF),
            pltpu.VMEM((layers, 2, 2 * xy, cols), BF),
            pltpu.VMEM((nctx // 4, 2, 4, 2 * xy, cols), BF),
            pltpu.VMEM(send.shape, BF),
            pltpu.VMEM(send.shape, BF),
            dma((xy,)),
            dma((xy,)),
            dma((2, layers, 2)),
            dma((layers, 2)),
            dma((2, layers, 2)),
            dma((seg, 2)),
            dma((layers, 2)),
            dma((layers, 2)),
            dma((2, layers, 2)),
            dma((2, nctx)),
            dma((2, nctx)),
            dma((2, nctx)),
            dma((2 * layers,)),
            dma((2 * layers,)),
            dma((xy,)),
            dma((xy,)),
        ],
        compiler_params=pltpu.CompilerParams(
            collective_id=1, has_side_effects=True, vmem_limit_bytes=48 << 20
        ),
    )(send, wgu, wd)


def join_kernel(experts, att_ref, back_ref, comb_ref, idr_ref, idc_ref, out_ref):
    tok, width = att_ref.shape
    count, span = back_ref.shape
    idr = idr_ref[0:1]
    idc = idc_ref[...]
    before = lax.broadcasted_iota(jnp.int32, (tok, tok), 1) < lax.broadcasted_iota(
        jnp.int32, (tok, tok), 0
    )
    earlier = jnp.sum(
        jnp.where(jnp.logical_and(before, idc == idr), 1, 0), axis=1, keepdims=True
    )
    slot = slots(idc, earlier, experts)
    r = lax.broadcasted_iota(jnp.int32, (tok, count), 1)
    match = wanted_slot(r, count // 16) == slot
    part = quarter_of(r)
    comb = comb_ref[...]
    for q in range(4):
        chooser = jnp.where(jnp.logical_and(match, part == q), 1.0, 0.0).astype(BF)
        picked = jnp.dot(chooser, back_ref[...], preferred_element_type=F32)
        at = slice(q * span, (q + 1) * span)
        out_ref[:, at] = (att_ref[:, at].astype(F32) + comb * picked).astype(BF)


def join(att, back, comb, idr, idc, experts):
    vm = pl.BlockSpec(memory_space=pltpu.VMEM)
    return pl.pallas_call(
        functools.partial(join_kernel, experts),
        out_shape=jax.ShapeDtypeStruct(att.shape, BF),
        in_specs=[vm] * 5,
        out_specs=vm,
        compiler_params=pltpu.CompilerParams(vmem_limit_bytes=24 << 20),
    )(att, back, comb, idr, idc)


def shards(query, keyval, doc_ids, route_ids, combine, w_gate_up, w_down):
    nctx = lax.axis_size("ctx")
    nexp = lax.axis_size("exp")
    tok = query.shape[1]
    units = w_gate_up.shape[2]
    kv, doc = spread(keyval[0], jnp.broadcast_to(doc_ids, (8, tok)), nctx)
    idr = jnp.broadcast_to(route_ids, (8, tok))
    idc = route_ids.reshape(tok, 1)
    att, send = attend(kv, doc, query[0], doc_ids.reshape(tok, 1), idr, idc, nexp)
    back = run_experts(send, w_gate_up[0].reshape(2 * units, -1), w_down[0], nctx, nexp)
    return join(att, back, combine.reshape(tok, 1), idr, idc, nexp)[None]


def solution(mesh):
    placed = (
        P("exp", "ctx", None),
        P("exp", None, "ctx", None),
        P("exp", "ctx"),
        P("exp", "ctx"),
        P("exp", "ctx"),
        P("exp", None, "ctx", None),
        P("exp", None, "ctx"),
    )
    return jax.shard_map(
        shards, mesh=mesh, in_specs=placed, out_specs=P("exp", "ctx", None), check_vma=False
    )
```

```python
import functools

import jax
import jax.numpy as jnp
from jax import lax
from jax.experimental import pallas as pl
from jax.experimental.pallas import tpu as pltpu
from jax.sharding import PartitionSpec as P

HD = 128
CAP = 2
EPS = 1e-06
LOWEST = -1e30
LOG2E = 1.4426950408889634
REACH = 1024

BF = jnp.bfloat16
F32 = jnp.float32
MESH = pl.DeviceIdType.MESH
HBM = pltpu.HBM
NT = (((1,), (1,)), ((), ()))
TN = (((0,), (0,)), ((), ()))


def remote(src, dst, send_sem, recv_sem, target):
    return pltpu.make_async_remote_copy(
        src_ref=src,
        dst_ref=dst,
        send_sem=send_sem,
        recv_sem=recv_sem,
        device_id=target,
        device_id_type=MESH,
    )


def spread_kernel(
    nctx, kv_ref, doc_ref, w_ref, kv_out, doc_out, w_out,
    got, got_doc, sent, sent_doc, shown, shown_doc, kept, w_sent, w_got,
):
    tok = kv_ref.shape[1]
    seg = nctx // 2
    reach = min(seg - 1, -(-REACH // (2 * tok)))
    ctx = lax.axis_index("ctx")
    exp = lax.axis_index("exp")
    core = lax.rem(ctx, 2)
    pos = ctx // 2
    sibling = (ctx + 1 - 2 * core, exp)

    def block(b):
        return pl.ds(pl.multiple_of(b * tok, tok), tok)

    def neighbour(way):
        return (ctx + 2 * way, exp)

    def has(p):
        return jnp.logical_and(p >= 0, p < seg)

    barrier = pltpu.get_barrier_semaphore()
    pl.semaphore_signal(barrier, inc=1, device_id=sibling, device_id_type=MESH)
    for way in (1, -1):

        @pl.when(has(pos + way))
        def _():
            pl.semaphore_signal(barrier, inc=1, device_id=neighbour(way), device_id_type=MESH)

    pl.semaphore_wait(
        barrier, 1 + (pos > 0).astype(jnp.int32) + (pos < seg - 1).astype(jnp.int32)
    )

    def moves(b, sems, doc_sem, target, first):
        out = []
        for part in range(2):
            src = kv_ref.at[part] if first else kv_out.at[part, block(b)]
            out.append(
                remote(src, kv_out.at[part, block(b)], sems.at[part], got.at[b, part], target)
            )
        src = doc_ref.at[0:1] if first else doc_out.at[b]
        out.append(remote(src, doc_out.at[b], doc_sem, got_doc.at[b], target))
        return out

    def along(way, t, b):
        d = 0 if way == 1 else 1
        return moves(b, sent.at[d, t], sent_doc.at[d, t], neighbour(way), t == 0)

    def across(b, first):
        return moves(b, shown.at[b], shown_doc.at[b], sibling, first)

    for way in (1, -1):

        @pl.when(has(pos + way))
        def _():
            for copy in along(way, 0, ctx):
                copy.start()

    for copy in across(ctx, True):
        copy.start()
    idle = jnp.logical_or(pos == 0, pos == seg - 1)
    near = jnp.logical_or(pos == 1, pos == seg - 2)
    inwards = jnp.where(pos < seg // 2, ctx + 2, ctx - 2)
    early = w_out.shape[0] // 16

    def weights(i):
        part = pl.ds(i * 16, 16)
        return remote(w_ref.at[part], w_out.at[part], w_sent.at[i], w_got.at[i], (inwards, exp))

    @pl.when(idle)
    def _():
        for i in range(early):
            weights(i).start()

    own = [
        pltpu.make_async_copy(kv_ref, kv_out.at[:, block(ctx)], kept.at[0]),
        pltpu.make_async_copy(doc_ref, doc_out.at[ctx], kept.at[1]),
    ]
    for copy in own:
        copy.start()

    for t in range(1, reach + 1):
        for way in (1, -1):
            source = pos - way * t
            b = 2 * source + core

            @pl.when(has(source))
            def _():
                there = across(b, False)
                on = along(way, t, b) if t < reach else None
                for n in range(3):
                    there[n].wait_recv()
                    if on is not None:

                        @pl.when(has(pos + way))
                        def _():
                            on[n].start()

                    there[n].start()

    for copy in own:
        copy.wait()

    @pl.when(idle)
    def _():
        for i in range(early):
            weights(i).wait_send()

    @pl.when(near)
    def _():
        for i in range(early):
            weights(i).wait_recv()

    for t in range(0, reach + 1):
        for way in (1, -1):
            source = pos - way * t
            b = 2 * source + core

            @pl.when(has(source))
            def _():
                if t > 0 or way == 1:
                    for copy in across(2 * source + 1 - core, False):
                        copy.wait_recv()
                    for copy in across(b, False):
                        copy.wait_send()
                if t < reach:

                    @pl.when(has(pos + way))
                    def _():
                        for copy in along(way, t, b):
                            copy.wait_send()


def spread(kv, doc, wgu, nctx):
    early = max(1, wgu.shape[0] // 16 * 5 // 12)
    _, tok, width = kv.shape
    return pl.pallas_call(
        functools.partial(spread_kernel, nctx),
        out_shape=(
            jax.ShapeDtypeStruct((2, nctx * tok, width), BF),
            jax.ShapeDtypeStruct((nctx, 1, tok), jnp.int32),
            jax.ShapeDtypeStruct((16 * early, wgu.shape[1]), BF),
        ),
        in_specs=[pl.BlockSpec(memory_space=HBM)] * 3,
        out_specs=(pl.BlockSpec(memory_space=pltpu.VMEM),) * 3,
        scratch_shapes=[
            pltpu.SemaphoreType.DMA((nctx, 2)),
            pltpu.SemaphoreType.DMA((nctx,)),
            pltpu.SemaphoreType.DMA((2, 8, 2)),
            pltpu.SemaphoreType.DMA((2, 8)),
            pltpu.SemaphoreType.DMA((nctx, 2)),
            pltpu.SemaphoreType.DMA((nctx,)),
            pltpu.SemaphoreType.DMA((2,)),
            pltpu.SemaphoreType.DMA((early,)),
            pltpu.SemaphoreType.DMA((early,)),
        ],
        compiler_params=pltpu.CompilerParams(
            collective_id=0, has_side_effects=True, vmem_limit_bytes=16 << 20
        ),
    )(kv, doc, wgu)


def wanted_slot(r, columns):
    d, i = r // 16, lax.rem(r, 4)
    return (columns * (i // 2) + d) * CAP + lax.rem(i, 2)


def quarter_of(r):
    return lax.rem(r, 16) // 4


def column(row):
    n = row.shape[1]
    return jnp.transpose(jnp.broadcast_to(row, (n, n)))[:, :1]


def slots(ids, earlier, experts):
    kept = jnp.logical_and(ids < experts, earlier < CAP)
    return jnp.where(kept, ids * CAP + earlier, -1)


def attend_kernel(
    experts, kv_ref, doc_ref, q_hbm, id_hbm, att_ref, send_ref, q_ref, id_ref, s_scr, m_scr, l_scr, a_scr, q_got
):
    tok, width = q_ref.shape
    nctx = doc_ref.shape[0]
    share = width // (kv_ref.shape[2] // HD)
    loads = [
        pltpu.make_async_copy(
            q_hbm.at[:, g * share : (g + 1) * share],
            q_ref.at[:, g * share : (g + 1) * share],
            q_got.at[g],
        )
        for g in range(width // share)
    ]
    loads.append(pltpu.make_async_copy(id_hbm, id_ref, q_got.at[len(loads)]))
    for load in loads:
        load.start()
    groups = kv_ref.shape[2] // HD
    per = width // HD // groups
    step = 2 * tok
    seg = nctx // 2
    reach = min(seg - 1, -(-REACH // step))
    pos = lax.axis_index("ctx") // 2
    scale = HD ** (-0.5) * LOG2E

    where = lax.broadcasted_iota(jnp.int32, (nctx, 1, tok), 0) // 2
    docs = jnp.where(where < pos - reach, -1, jnp.where(where > pos + reach, 1 << 20, doc_ref[...]))
    qdoc = doc_ref[lax.axis_index("ctx")]
    low = jnp.min(qdoc)
    high = jnp.max(qdoc)
    begin = jnp.sum((docs < low).astype(jnp.int32))
    end = jnp.sum((docs <= high).astype(jnp.int32))
    qdoc = column(qdoc)
    first = begin // step
    last = (end + step - 1) // step

    squares = jnp.zeros((tok, HD), F32)
    for g in range(groups):
        lanes = slice(g * HD, (g + 1) * HD)
        loads[g].wait()
        m_scr[...] = jnp.full(m_scr.shape, LOWEST, F32)
        l_scr[...] = jnp.zeros(l_scr.shape, F32)
        a_scr[...] = jnp.zeros(a_scr.shape, F32)

        @pl.loop(first, last)
        def _(kb):
            keys = kv_ref[0, pl.ds(pl.multiple_of(kb * step, step), step), lanes]
            kdoc = jnp.concatenate([doc_ref[2 * kb, 0:1], doc_ref[2 * kb + 1, 0:1]], axis=1)
            bias = jnp.where(kdoc == qdoc, 0.0, LOWEST).astype(F32)
            for h in range(per):
                at = slice((g * per + h) * HD, (g * per + h + 1) * HD)
                rows = slice(h * tok, (h + 1) * tok)
                s = lax.dot_general(q_ref[:, at], keys, NT, preferred_element_type=F32) + bias
                s_scr[kb, rows] = s
                m_scr[rows] = jnp.maximum(
                    m_scr[rows], jnp.maximum(s[:, :HD], s[:, HD:])
                )

        for h in range(per):
            rows = slice(h * tok, (h + 1) * tok)
            m_scr[rows] = jnp.broadcast_to(
                jnp.max(m_scr[rows], axis=1, keepdims=True), (tok, HD)
            )

        @pl.loop(first, last)
        def _(kb):
            values = kv_ref[1, pl.ds(pl.multiple_of(kb * step, step), step), lanes]
            for h in range(per):
                rows = slice(h * tok, (h + 1) * tok)
                top = m_scr[rows]
                s = s_scr[kb, rows]
                p = jnp.exp2((s - jnp.concatenate([top, top], axis=1)) * scale)
                l_scr[rows] = l_scr[rows] + (p[:, :HD] + p[:, HD:])
                a_scr[rows] = a_scr[rows] + jnp.dot(
                    p.astype(BF), values, preferred_element_type=F32
                )

        for h in range(per):
            at = slice((g * per + h) * HD, (g * per + h + 1) * HD)
            rows = slice(h * tok, (h + 1) * tok)
            total = jnp.sum(l_scr[rows], axis=1, keepdims=True)
            mixed = (a_scr[rows] / total).astype(BF)
            att_ref[:, at] = mixed
            wide = mixed.astype(F32)
            squares = squares + wide * wide

    loads[-1].wait()
    inverse = lax.rsqrt(jnp.sum(squares, axis=1, keepdims=True) / width + EPS)
    idr = id_ref[...]
    idc = column(idr)
    before = lax.broadcasted_iota(jnp.int32, (tok, tok), 0) < lax.broadcasted_iota(
        jnp.int32, (tok, tok), 1
    )
    earlier = jnp.sum(
        jnp.where(jnp.logical_and(before, idc == idr), 1, 0), axis=0, keepdims=True
    )
    slot = slots(idr, earlier, experts)
    count = send_ref.shape[0]
    r = lax.broadcasted_iota(jnp.int32, (count, tok), 0)
    match = wanted_slot(r, count // 16) == slot
    part = quarter_of(r)
    span = width // 4
    for piece in range(0, span, 256):
        total = jnp.zeros((count, 256), F32)
        for q in range(4):
            chooser = jnp.where(jnp.logical_and(match, part == q), 1.0, 0.0).astype(BF)
            att = att_ref[:, q * span + piece : q * span + piece + 256].astype(F32)
            normed = (att * inverse).astype(BF)
            total = total + jnp.dot(chooser, normed, preferred_element_type=F32)
        send_ref[:, piece : piece + 256] = total.astype(BF)


def attend(kv, doc, q, ids, experts):
    tok, width = q.shape
    nctx = doc.shape[0]
    per = width // HD // (kv.shape[2] // HD)
    count = 16 * (experts // 2)
    vm = pl.BlockSpec(memory_space=pltpu.VMEM)
    return pl.pallas_call(
        functools.partial(attend_kernel, experts),
        out_shape=(
            jax.ShapeDtypeStruct((tok, width), BF),
            jax.ShapeDtypeStruct((count, width // 4), BF),
        ),
        in_specs=[vm, vm] + [pl.BlockSpec(memory_space=HBM)] * 2,
        out_specs=(vm, vm),
        scratch_shapes=[
            pltpu.VMEM((tok, width), BF),
            pltpu.VMEM((1, tok), jnp.int32),
            pltpu.VMEM((nctx // 2, per * tok, 2 * tok), F32),
            pltpu.VMEM((per * tok, HD), F32),
            pltpu.VMEM((per * tok, HD), F32),
            pltpu.VMEM((per * tok, HD), F32),
            pltpu.SemaphoreType.DMA((width // HD // per + 1,)),
        ],
        compiler_params=pltpu.CompilerParams(vmem_limit_bytes=48 << 20),
    )(kv, doc, q, ids)


def experts_kernel(
    nctx, nexp, send_ref, wgu_ref, wd_ref, early_ref, back_ref,
    came, rows, transit, hid0, hid1, made, ret, send2, back,
    a_sent, a_got, r_sent, r_got, t_sent, t_got, x_sent, x_got,
    h_sent, h_got, y_sent, y_got, d_sent, d_got, b_sent, b_got, wx, w_sent, w_got,
):
    seg = nctx // 2
    half = seg // 2
    xy = nexp // 2
    span = send_ref.shape[1]
    width = 4 * span
    piece = xy
    units = wgu_ref.shape[0] // 2
    cols = wd_ref.shape[1]
    ctx = lax.axis_index("ctx")
    exp = lax.axis_index("exp")
    core = lax.rem(ctx, 2)
    pos = ctx // 2
    zhi = exp // xy
    place = lax.rem(exp, xy)
    layer = zhi * seg + pos
    layers = 2 * seg
    sibling = (ctx + 1 - 2 * core, exp)

    idle = jnp.logical_or(pos == 0, pos == seg - 1)
    near = jnp.logical_or(pos == 1, pos == seg - 2)
    beside = jnp.where(pos < half, ctx + 2, ctx - 2)
    outer = jnp.where(pos < half, ctx - 2, ctx + 2)
    parts = 2 * units // 16
    early = early_ref.shape[0] // 16
    ahead = early + min(parts // 3, parts - early)

    def weights(i, target):
        part = pl.ds(pl.multiple_of(i * 16, 16), 16)
        return remote(wgu_ref.at[part], wx.at[part], w_sent.at[i], w_got.at[i], (target, exp))

    def at_layer(z, c):
        z = lax.rem(z + 2 * layers, layers)
        return (2 * lax.rem(z, seg) + c, (z // seg) * xy + place)

    def at_place(d):
        return (ctx, zhi * xy + d)

    barrier = pltpu.get_barrier_semaphore()

    @pl.loop(1, xy)
    def _(j):
        pl.semaphore_signal(
            barrier, inc=1, device_id=at_place(lax.rem(place + j, xy)), device_id_type=MESH
        )

    @pl.loop(1, 2 * layers)
    def _(j):
        me = 2 * layer + core
        n = lax.rem(me + j, 2 * layers)
        pl.semaphore_signal(
            barrier, inc=1, device_id=at_layer(n // 2, lax.rem(n, 2)), device_id_type=MESH
        )

    pl.semaphore_wait(barrier, xy - 1 + 2 * layers - 1)

    def block16(d):
        return pl.ds(pl.multiple_of(d * 16, 16), 16)

    def swap(src, dst, sent, got, d):
        out = remote(src.at[block16(d)], dst.at[block16(place)], sent.at[d], got.at[place], at_place(d))
        into = remote(src.at[block16(place)], dst.at[block16(d)], sent.at[place], got.at[d], at_place(d))
        return out, into

    def exchange(src, dst, sent, got):
        @pl.loop(1, xy)
        def _(j):
            swap(src, dst, sent, got, lax.rem(place + j, xy))[0].start()

        dst[block16(place)] = src[block16(place)]

        @pl.loop(1, xy)
        def _(j):
            swap(src, dst, sent, got, lax.rem(place + xy - j, xy))[1].wait_recv()

    def exchange_end(src, dst, sent, got):
        @pl.loop(1, xy)
        def _(j):
            swap(src, dst, sent, got, lax.rem(place + j, xy))[0].wait_send()

    @pl.when(idle)
    def _():
        for i in range(early, ahead):
            weights(i, beside).start()

    @pl.when(near)
    def _():
        wx[: 16 * early] = early_ref[...]

    exchange(send_ref, came, a_sent, a_got)
    r = lax.broadcasted_iota(jnp.int32, (2 * xy, 16 * xy), 0)
    c = lax.broadcasted_iota(jnp.int32, (2 * xy, 16 * xy), 1)
    for side in range(2):
        z = zhi if side == 0 else 1 - zhi
        for q in range(4):
            pick = jnp.where(
                c == (r // 2) * 16 + q * 4 + 2 * z + lax.rem(r, 2), 1.0, 0.0
            ).astype(BF)
            got = jnp.dot(pick, came[...], preferred_element_type=F32).astype(BF)
            for h in range(2):
                kept = got[h * piece : (h + 1) * piece]
                if side == 0:
                    rows[layer, core, h, :, q * span : (q + 1) * span] = kept
                else:
                    transit[pos, h, :, q * span : (q + 1) * span] = kept

    def ring(z):
        return lax.rem(z + 2 * layers, layers)

    def rank_of(way):
        return pos if way == 1 else seg - 1 - pos

    def chunk_moves(way, t, h):
        d = 0 if way == 1 else 1
        k = rank_of(way)
        z = ring(layer - way * (t - 1))
        p = lax.rem(pos - way * (t - 1) + 2 * seg, seg)
        target = at_layer(layer + way, core)
        return [
            (
                jnp.logical_and(k < seg - 1, t <= k + 1 - half),
                remote(transit.at[p, h], transit.at[p, h], t_sent.at[d, t, h], t_got.at[p, h], target),
            ),
            (
                jnp.logical_and(k == seg - 1, t <= half),
                remote(transit.at[p, h], rows.at[z, core, h], t_sent.at[d, t, h], r_got.at[z, h], target),
            ),
            (
                jnp.logical_and(k < seg - 2, t <= k + 1 + half),
                remote(rows.at[z, core, h], rows.at[z, core, h], r_sent.at[d, t, h], r_got.at[z, h], target),
            ),
        ]

    def chunk_start(way, t, h):
        for cond, copy in chunk_moves(way, t, h):

            @pl.when(cond)
            def _():
                copy.start()

    def show(z, h, c):
        return remote(rows.at[z, c, h], rows.at[z, c, h], x_sent.at[z, h], x_got.at[z, h], sibling)

    for h in range(2):
        for way in (1, -1):
            chunk_start(way, 1, h)
        pl.when(jnp.logical_not(idle))(show(layer, h, core).start)

    steps = seg - 2 + half

    def rows_step(t):
        for j in range(2):
            i = ahead + 2 * (t - 1) + j

            @pl.when(jnp.logical_and(idle, i < parts))
            def _():
                weights(i, beside).start()

        for h in range(2):
            for way in (1, -1):
                k = rank_of(way)
                z = ring(layer - way * t)
                p = lax.rem(pos - way * t + 2 * seg, seg)

                @pl.when(t <= k - half)
                def _():
                    remote(
                        transit.at[p, h], transit.at[p, h], t_sent.at[0, 0, h], t_got.at[p, h], sibling
                    ).wait_recv()

                needed = jnp.logical_and(k < seg - 1, t <= k + half)

                @pl.when(needed)
                def _():
                    remote(
                        rows.at[z, core, h], rows.at[z, core, h], r_sent.at[0, 0, h], r_got.at[z, h], sibling
                    ).wait_recv()

                chunk_start(way, t + 1, h)

                @pl.when(jnp.logical_and(needed, jnp.logical_not(idle)))
                def _():
                    show(z, h, core).start()

    mine, other = zhi, 1 - zhi
    quart = half // 2
    sizes = (seg, half, half)

    def layer_of(g, j):
        if g == 0:
            return mine * seg + j
        if g == 1:
            return other * seg + j + jnp.where(j >= quart, seg - half, 0)
        return other * seg + quart + j

    def ranges(g):
        if g == 0:
            return [(mine * seg, seg, 0)]
        if g == 1:
            return [(other * seg, quart, 0), (other * seg + seg - quart, quart, quart)]
        return [(other * seg + quart, half, 0)]

    def rows_shown(g):
        @pl.when(jnp.logical_not(idle))
        def _():
            @pl.loop(0, sizes[g])
            def _(j):
                for h in range(2):
                    show(layer_of(g, j), h, 1 - core).wait_recv()

    def hid(g, b):
        return hid0.at[b] if g == 0 else hid1.at[g - 1, b]

    def hid_move(g, b, sent, target):
        return remote(hid(g, b), hid(g, b), sent, h_got.at[g, b], target)

    def hid_came(g, b):
        hid_move(g, b, h_sent.at[0, 0, g], sibling).wait_recv()

    def hid_moves(way, t, g):
        d = 0 if way == 1 else 1
        k = rank_of(way)
        b = 2 * (pos - way * (t - 1)) + core
        return (
            jnp.logical_and(jnp.logical_and(k > 0, k < seg - 1), t <= k + 1),
            hid_move(g, b, h_sent.at[d, t, g], (ctx + 2 * way, exp)),
        )

    def hid_start(way, t, g):
        cond, copy = hid_moves(way, t, g)

        @pl.when(cond)
        def _():
            copy.start()

    def hid_show(g, b):
        return remote(hid(g, b), hid(g, b), y_sent.at[g, b], y_got.at[g, b], sibling)

    chunk = 4 * xy

    def hid_out(way, g):
        d = 0 if way == 1 else 1
        return hid_move(g, outer, h_sent.at[d, 0, g], (outer, exp))

    def units_of(w, g):
        x = [rows[pl.ds(z, n)].reshape(n * chunk, width) for z, n, _ in ranges(g)]
        x = x[0] if len(x) == 1 else jnp.concatenate(x, axis=0)
        both = lax.dot_general(w[...], x, NT, preferred_element_type=F32)
        gate, upper = both[:units], both[units:]
        return (gate / (1.0 + jnp.exp(-gate)) * upper).astype(BF)

    def gate_up(g):
        rows_shown(g)

        @pl.when(jnp.logical_not(idle))
        def _():
            hid(g, ctx)[...] = units_of(wgu_ref, g)
            for way in (1, -1):
                hid_start(way, 1, g)
            hid_show(g, ctx).start()

        @pl.when(near)
        def _():
            if g == 0:

                @pl.loop(early, parts)
                def _(i):
                    weights(i, outer).wait_recv()

            hid(g, outer)[...] = units_of(wx, g)
            for way in (1, -1):

                @pl.when(rank_of(way) == 1)
                def _():
                    hid_out(way, g).start()
                    hid_start(way, 2, g)

            hid_show(g, outer).start()

    def hid_step(g, t):
        @pl.when(jnp.logical_and(idle, t == 1))
        def _():
            hid_came(g, ctx)
            hid_show(g, ctx).start()

        for way in (1, -1):
            k = rank_of(way)
            b = 2 * (pos - way * t) + core

            @pl.when(jnp.logical_and(t <= k, k + t > 2))
            def _():
                hid_came(g, b)
                hid_start(way, t + 1, g)
                hid_show(g, b).start()

    fold = nctx // 4

    def home(z, c):
        slot = (lax.rem(ctx, fold), zhi, ctx // fold)
        n = zhi * nctx + ctx
        return remote(
            made.at[z, c], ret.at[slot], d_sent.at[2 * z + c], d_got.at[n], at_layer(z, c)
        )

    def home_from(z, c):
        n_ctx = 2 * lax.rem(z, seg) + c
        n = (z // seg) * nctx + n_ctx
        slot = (lax.rem(n_ctx, fold), z // seg, n_ctx // fold)
        return remote(made.at[z, c], ret.at[slot], d_sent.at[2 * z + c], d_got.at[n], at_layer(z, c))

    def down(g):
        @pl.loop(0, seg)
        def _(p):
            hid_show(g, 2 * p + 1 - core).wait_recv()

        some = sizes[g] * chunk
        hidden = (hid0[...] if g == 0 else hid1[g - 1]).reshape(nctx * units, some)
        out = lax.dot_general(hidden, wd_ref[...], TN, preferred_element_type=F32)
        out = out.astype(BF).reshape(sizes[g], 2, 2 * xy, cols)
        for z, n, j in ranges(g):
            made[pl.ds(z, n)] = out[j : j + n]
        count = 2 * sizes[g]

        @pl.loop(0, count)
        def _(j):
            n = lax.rem(ctx + j, count)
            z, c = layer_of(g, n // 2), lax.rem(n, 2)

            @pl.when(jnp.logical_or(z != layer, c != core))
            def _():
                home(z, c).start()

    @pl.loop(1, seg - 1)
    def _(t):
        rows_step(t)

    gate_up(0)

    @pl.loop(1, quart + 1)
    def _(u):
        rows_step(seg - 2 + u)
        hid_step(0, u)

    gate_up(1)

    @pl.loop(quart + 1, half + 1)
    def _(u):
        rows_step(seg - 2 + u)
        hid_step(0, u)
        hid_step(1, u - quart)

    gate_up(2)

    @pl.loop(half + 1, seg)
    def _(u):
        hid_step(0, u)
        hid_step(1, u - quart)
        hid_step(2, u - half)

    down(0)

    @pl.loop(seg, seg + quart)
    def _(u):
        hid_step(1, u - quart)
        hid_step(2, u - half)

    down(1)

    @pl.loop(seg + quart, seg + half)
    def _(u):
        hid_step(2, u - half)

    down(2)

    ret[lax.rem(ctx, fold), zhi, ctx // fold] = made[layer, core]

    @pl.loop(1, 2 * layers)
    def _(j):
        n = lax.rem(2 * layer + core + j, 2 * layers)
        home_from(n // 2, lax.rem(n, 2)).wait_recv()

    r = lax.broadcasted_iota(jnp.int32, (16 * xy, 16 * xy), 0)
    c = lax.broadcasted_iota(jnp.int32, (16 * xy, 16 * xy), 1)
    i = lax.rem(r, 4)
    place_back = jnp.where(
        c == ((i // 2) * 4 + quarter_of(r)) * 2 * xy + 2 * (r // 16) + lax.rem(i, 2), 1.0, 0.0
    ).astype(BF)
    for m in range(fold):
        got = ret[m].reshape(16 * xy, cols)
        send2[:, m * cols : (m + 1) * cols] = jnp.dot(
            place_back, got, preferred_element_type=F32
        ).astype(BF)
    exchange(send2, back, b_sent, b_got)
    back_ref[...] = back[...]

    exchange_end(send_ref, came, a_sent, a_got)
    exchange_end(send2, back, b_sent, b_got)

    @pl.loop(1, steps + 2)
    def _(t):
        for h in range(2):
            for way in (1, -1):
                for cond, copy in chunk_moves(way, t, h):

                    @pl.when(cond)
                    def _():
                        copy.wait_send()

    @pl.when(jnp.logical_not(idle))
    def _():
        @pl.loop(0, layers)
        def _(z):
            for h in range(2):
                show(z, h, core).wait_send()

    @pl.when(idle)
    def _():
        @pl.loop(early, parts)
        def _(i):
            weights(i, beside).wait_send()

    for way in (1, -1):
        for g in range(3):
            pl.when(rank_of(way) == 1)(hid_out(way, g).wait_send)

    @pl.loop(1, seg + 1)
    def _(t):
        for g in range(3):
            for way in (1, -1):
                cond, copy = hid_moves(way, t, g)

                @pl.when(cond)
                def _():
                    copy.wait_send()

    @pl.loop(0, seg)
    def _(p):
        for g in range(3):
            hid_show(g, 2 * p + core).wait_send()

    @pl.loop(1, 2 * layers)
    def _(j):
        n = lax.rem(2 * layer + core + j, 2 * layers)
        home(n // 2, lax.rem(n, 2)).wait_send()


def run_experts(send, wgu, wd, wx, nctx, nexp):
    xy = nexp // 2
    seg = nctx // 2
    layers = 2 * seg
    span = send.shape[1]
    width = 4 * span
    units = wgu.shape[0] // 2
    cols = wd.shape[1]
    dma = pltpu.SemaphoreType.DMA
    vm = pl.BlockSpec(memory_space=pltpu.VMEM)
    return pl.pallas_call(
        functools.partial(experts_kernel, nctx, nexp),
        out_shape=jax.ShapeDtypeStruct(send.shape, BF),
        in_specs=[vm] * 4,
        out_specs=vm,
        scratch_shapes=[
            pltpu.VMEM(send.shape, BF),
            pltpu.VMEM((layers, 2, 2, xy, width), BF),
            pltpu.VMEM((seg, 2, xy, width), BF),
            pltpu.VMEM((nctx, units, seg * 4 * xy), BF),
            pltpu.VMEM((2, nctx, units, seg * 2 * xy), BF),
            pltpu.VMEM((layers, 2, 2 * xy, cols), BF),
            pltpu.VMEM((nctx // 4, 2, 4, 2 * xy, cols), BF),
            pltpu.VMEM(send.shape, BF),
            pltpu.VMEM(send.shape, BF),
            dma((xy,)),
            dma((xy,)),
            dma((2, layers, 2)),
            dma((layers, 2)),
            dma((2, layers, 2)),
            dma((seg, 2)),
            dma((layers, 2)),
            dma((layers, 2)),
            dma((2, layers, 3)),
            dma((3, nctx)),
            dma((3, nctx)),
            dma((3, nctx)),
            dma((2 * layers,)),
            dma((2 * layers,)),
            dma((xy,)),
            dma((xy,)),
            pltpu.VMEM(wgu.shape, BF),
            dma((2 * units // 16,)),
            dma((2 * units // 16,)),
        ],
        compiler_params=pltpu.CompilerParams(
            collective_id=1, has_side_effects=True, vmem_limit_bytes=48 << 20
        ),
    )(send, wgu, wd, wx)


def join_kernel(experts, att_ref, back_ref, comb_hbm, id_hbm, out_ref, comb_ref, id_ref, got):
    loads = [
        pltpu.make_async_copy(comb_hbm, comb_ref, got.at[0]),
        pltpu.make_async_copy(id_hbm, id_ref, got.at[1]),
    ]
    for load in loads:
        load.start()
    for load in loads:
        load.wait()
    tok, width = att_ref.shape
    count, span = back_ref.shape
    idr = id_ref[...]
    idc = column(idr)
    before = lax.broadcasted_iota(jnp.int32, (tok, tok), 1) < lax.broadcasted_iota(
        jnp.int32, (tok, tok), 0
    )
    earlier = jnp.sum(
        jnp.where(jnp.logical_and(before, idc == idr), 1, 0), axis=1, keepdims=True
    )
    slot = slots(idc, earlier, experts)
    r = lax.broadcasted_iota(jnp.int32, (tok, count), 1)
    match = wanted_slot(r, count // 16) == slot
    part = quarter_of(r)
    comb = column(comb_ref[...])
    for q in range(4):
        chooser = jnp.where(jnp.logical_and(match, part == q), 1.0, 0.0).astype(BF)
        picked = jnp.dot(chooser, back_ref[...], preferred_element_type=F32)
        at = slice(q * span, (q + 1) * span)
        out_ref[:, at] = (att_ref[:, at].astype(F32) + comb * picked).astype(BF)


def join(att, back, comb, ids, experts):
    vm = pl.BlockSpec(memory_space=pltpu.VMEM)
    return pl.pallas_call(
        functools.partial(join_kernel, experts),
        out_shape=jax.ShapeDtypeStruct(att.shape, BF),
        in_specs=[vm, vm] + [pl.BlockSpec(memory_space=HBM)] * 2,
        out_specs=vm,
        scratch_shapes=[
            pltpu.VMEM(comb.shape, F32),
            pltpu.VMEM(ids.shape, jnp.int32),
            pltpu.SemaphoreType.DMA((2,)),
        ],
        compiler_params=pltpu.CompilerParams(vmem_limit_bytes=24 << 20),
    )(att, back, comb, ids)


def shards(query, keyval, doc_ids, route_ids, combine, w_gate_up, w_down):
    nctx = lax.axis_size("ctx")
    nexp = lax.axis_size("exp")
    units = w_gate_up.shape[2]
    wgu = w_gate_up[0].reshape(2 * units, -1)
    kv, doc, wx = spread(keyval[0], doc_ids, wgu, nctx)
    att, send = attend(kv, doc, query[0], route_ids, nexp)
    back = run_experts(send, wgu, w_down[0], wx, nctx, nexp)
    return join(att, back, combine, route_ids, nexp)[None]


def solution(mesh):
    placed = (
        P("exp", "ctx", None),
        P("exp", None, "ctx", None),
        P("exp", "ctx"),
        P("exp", "ctx"),
        P("exp", "ctx"),
        P("exp", None, "ctx", None),
        P("exp", None, "ctx"),
    )
    return jax.shard_map(
        shards, mesh=mesh, in_specs=placed, out_specs=P("exp", "ctx", None), check_vma=False
    )
```

```python
import functools

import jax
import jax.numpy as jnp
from jax import lax
from jax.experimental import pallas as pl
from jax.experimental.pallas import tpu as pltpu
from jax.sharding import PartitionSpec as P

HD = 128
CAP = 2
EPS = 1e-06
LOWEST = -1e30
LOG2E = 1.4426950408889634
REACH = 1024

BF = jnp.bfloat16
F32 = jnp.float32
MESH = pl.DeviceIdType.MESH
HBM = pltpu.HBM
NT = (((1,), (1,)), ((), ()))
TN = (((0,), (0,)), ((), ()))


def remote(src, dst, send_sem, recv_sem, target):
    return pltpu.make_async_remote_copy(
        src_ref=src,
        dst_ref=dst,
        send_sem=send_sem,
        recv_sem=recv_sem,
        device_id=target,
        device_id_type=MESH,
    )


def spread_kernel(
    nctx, kv_ref, doc_ref, w_ref, kv_out, doc_out, w_out,
    got, got_doc, sent, sent_doc, shown, shown_doc, kept, w_sent, w_got,
):
    tok = kv_ref.shape[1]
    seg = nctx // 2
    reach = min(seg - 1, -(-REACH // (2 * tok)))
    ctx = lax.axis_index("ctx")
    exp = lax.axis_index("exp")
    core = lax.rem(ctx, 2)
    pos = ctx // 2
    sibling = (ctx + 1 - 2 * core, exp)

    def block(b):
        return pl.ds(pl.multiple_of(b * tok, tok), tok)

    def neighbour(way):
        return (ctx + 2 * way, exp)

    def has(p):
        return jnp.logical_and(p >= 0, p < seg)

    barrier = pltpu.get_barrier_semaphore()
    pl.semaphore_signal(barrier, inc=1, device_id=sibling, device_id_type=MESH)
    for way in (1, -1):

        @pl.when(has(pos + way))
        def _():
            pl.semaphore_signal(barrier, inc=1, device_id=neighbour(way), device_id_type=MESH)

    pl.semaphore_wait(
        barrier, 1 + (pos > 0).astype(jnp.int32) + (pos < seg - 1).astype(jnp.int32)
    )

    def moves(b, sems, doc_sem, target, first):
        out = []
        for part in range(2):
            src = kv_ref.at[part] if first else kv_out.at[part, block(b)]
            out.append(
                remote(src, kv_out.at[part, block(b)], sems.at[part], got.at[b, part], target)
            )
        src = doc_ref.at[0:1] if first else doc_out.at[b]
        out.append(remote(src, doc_out.at[b], doc_sem, got_doc.at[b], target))
        return out

    def along(way, t, b):
        d = 0 if way == 1 else 1
        return moves(b, sent.at[d, t], sent_doc.at[d, t], neighbour(way), t == 0)

    def across(b, first):
        return moves(b, shown.at[b], shown_doc.at[b], sibling, first)

    for way in (1, -1):

        @pl.when(has(pos + way))
        def _():
            for copy in along(way, 0, ctx):
                copy.start()

    for copy in across(ctx, True):
        copy.start()
    idle = jnp.logical_or(pos == 0, pos == seg - 1)
    near = jnp.logical_or(pos == 1, pos == seg - 2)
    inwards = jnp.where(pos < seg // 2, ctx + 2, ctx - 2)
    early = w_out.shape[0] // 16

    def weights(i):
        part = pl.ds(i * 16, 16)
        return remote(w_ref.at[part], w_out.at[part], w_sent.at[i], w_got.at[i], (inwards, exp))

    @pl.when(idle)
    def _():
        for i in range(early):
            weights(i).start()

    own = [
        pltpu.make_async_copy(kv_ref, kv_out.at[:, block(ctx)], kept.at[0]),
        pltpu.make_async_copy(doc_ref, doc_out.at[ctx], kept.at[1]),
    ]
    for copy in own:
        copy.start()

    def finish(t):
        for way in (1, -1):
            source = pos - way * t
            b = 2 * source + core

            @pl.when(has(source))
            def _():
                if t > 0 or way == 1:
                    for copy in across(2 * source + 1 - core, False):
                        copy.wait_recv()
                    for copy in across(b, False):
                        copy.wait_send()
                if t < reach:

                    @pl.when(has(pos + way))
                    def _():
                        for copy in along(way, t, b):
                            copy.wait_send()

    for t in range(1, reach + 1):
        for way in (1, -1):
            source = pos - way * t
            b = 2 * source + core

            @pl.when(has(source))
            def _():
                there = across(b, False)
                on = along(way, t, b) if t < reach else None
                for n in range(3):
                    there[n].wait_recv()
                    if on is not None:

                        @pl.when(has(pos + way))
                        def _():
                            on[n].start()

                    there[n].start()

        if t >= 2:
            finish(t - 2)

    for copy in own:
        copy.wait()

    @pl.when(idle)
    def _():
        for i in range(early):
            weights(i).wait_send()

    @pl.when(near)
    def _():
        for i in range(early):
            weights(i).wait_recv()

    for t in range(max(0, reach - 1), reach + 1):
        finish(t)


def spread(kv, doc, wgu, nctx):
    early = max(1, wgu.shape[0] // 16 * 5 // 12)
    _, tok, width = kv.shape
    return pl.pallas_call(
        functools.partial(spread_kernel, nctx),
        out_shape=(
            jax.ShapeDtypeStruct((2, nctx * tok, width), BF),
            jax.ShapeDtypeStruct((nctx, 1, tok), jnp.int32),
            jax.ShapeDtypeStruct((16 * early, wgu.shape[1]), BF),
        ),
        in_specs=[pl.BlockSpec(memory_space=HBM)] * 3,
        out_specs=(pl.BlockSpec(memory_space=pltpu.VMEM),) * 3,
        scratch_shapes=[
            pltpu.SemaphoreType.DMA((nctx, 2)),
            pltpu.SemaphoreType.DMA((nctx,)),
            pltpu.SemaphoreType.DMA((2, 8, 2)),
            pltpu.SemaphoreType.DMA((2, 8)),
            pltpu.SemaphoreType.DMA((nctx, 2)),
            pltpu.SemaphoreType.DMA((nctx,)),
            pltpu.SemaphoreType.DMA((2,)),
            pltpu.SemaphoreType.DMA((early,)),
            pltpu.SemaphoreType.DMA((early,)),
        ],
        compiler_params=pltpu.CompilerParams(
            collective_id=0, has_side_effects=True, vmem_limit_bytes=16 << 20
        ),
    )(kv, doc, wgu)


def wanted_slot(r, columns):
    d, i = r // 16, lax.rem(r, 4)
    return (columns * (i // 2) + d) * CAP + lax.rem(i, 2)


def quarter_of(r):
    return lax.rem(r, 16) // 4


def column(row):
    n = row.shape[1]
    return jnp.transpose(jnp.broadcast_to(row, (n, n)))[:, :1]


def slots(ids, earlier, experts):
    kept = jnp.logical_and(ids < experts, earlier < CAP)
    return jnp.where(kept, ids * CAP + earlier, -1)


def attend_kernel(
    experts, kv_ref, doc_ref, q_hbm, id_hbm, att_ref, send_ref, q_ref, id_ref, s_scr, m_scr, l_scr, a_scr, q_got
):
    tok, width = q_ref.shape
    nctx = doc_ref.shape[0]
    share = width // (kv_ref.shape[2] // HD)
    loads = [
        pltpu.make_async_copy(
            q_hbm.at[:, g * share : (g + 1) * share],
            q_ref.at[:, g * share : (g + 1) * share],
            q_got.at[g],
        )
        for g in range(width // share)
    ]
    loads.append(pltpu.make_async_copy(id_hbm, id_ref, q_got.at[len(loads)]))
    for load in loads:
        load.start()
    groups = kv_ref.shape[2] // HD
    per = width // HD // groups
    step = 2 * tok
    seg = nctx // 2
    reach = min(seg - 1, -(-REACH // step))
    pos = lax.axis_index("ctx") // 2
    scale = HD ** (-0.5) * LOG2E

    where = lax.broadcasted_iota(jnp.int32, (nctx, 1, tok), 0) // 2
    docs = jnp.where(where < pos - reach, -1, jnp.where(where > pos + reach, 1 << 20, doc_ref[...]))
    qdoc = doc_ref[lax.axis_index("ctx")]
    low = jnp.min(qdoc)
    high = jnp.max(qdoc)
    begin = jnp.sum((docs < low).astype(jnp.int32))
    end = jnp.sum((docs <= high).astype(jnp.int32))
    qdoc = column(qdoc)
    first = begin // step
    last = (end + step - 1) // step

    squares = jnp.zeros((tok, HD), F32)
    for g in range(groups):
        lanes = slice(g * HD, (g + 1) * HD)
        loads[g].wait()
        m_scr[...] = jnp.full(m_scr.shape, LOWEST, F32)
        l_scr[...] = jnp.zeros(l_scr.shape, F32)
        a_scr[...] = jnp.zeros(a_scr.shape, F32)

        @pl.loop(first, last)
        def _(kb):
            keys = kv_ref[0, pl.ds(pl.multiple_of(kb * step, step), step), lanes]
            kdoc = jnp.concatenate([doc_ref[2 * kb, 0:1], doc_ref[2 * kb + 1, 0:1]], axis=1)
            bias = jnp.where(kdoc == qdoc, 0.0, LOWEST).astype(F32)
            for h in range(per):
                at = slice((g * per + h) * HD, (g * per + h + 1) * HD)
                rows = slice(h * tok, (h + 1) * tok)
                s = lax.dot_general(q_ref[:, at], keys, NT, preferred_element_type=F32) + bias
                s_scr[kb, rows] = s
                m_scr[rows] = jnp.maximum(
                    m_scr[rows], jnp.maximum(s[:, :HD], s[:, HD:])
                )

        for h in range(per):
            rows = slice(h * tok, (h + 1) * tok)
            m_scr[rows] = jnp.broadcast_to(
                jnp.max(m_scr[rows], axis=1, keepdims=True), (tok, HD)
            )

        @pl.loop(first, last)
        def _(kb):
            values = kv_ref[1, pl.ds(pl.multiple_of(kb * step, step), step), lanes]
            for h in range(per):
                rows = slice(h * tok, (h + 1) * tok)
                top = m_scr[rows]
                s = s_scr[kb, rows]
                p = jnp.exp2((s - jnp.concatenate([top, top], axis=1)) * scale)
                l_scr[rows] = l_scr[rows] + (p[:, :HD] + p[:, HD:])
                a_scr[rows] = a_scr[rows] + jnp.dot(
                    p.astype(BF), values, preferred_element_type=F32
                )

        for h in range(per):
            at = slice((g * per + h) * HD, (g * per + h + 1) * HD)
            rows = slice(h * tok, (h + 1) * tok)
            total = jnp.sum(l_scr[rows], axis=1, keepdims=True)
            mixed = (a_scr[rows] / total).astype(BF)
            att_ref[:, at] = mixed
            wide = mixed.astype(F32)
            squares = squares + wide * wide

    loads[-1].wait()
    inverse = lax.rsqrt(jnp.sum(squares, axis=1, keepdims=True) / width + EPS)
    idr = id_ref[...]
    idc = column(idr)
    before = lax.broadcasted_iota(jnp.int32, (tok, tok), 0) < lax.broadcasted_iota(
        jnp.int32, (tok, tok), 1
    )
    earlier = jnp.sum(
        jnp.where(jnp.logical_and(before, idc == idr), 1, 0), axis=0, keepdims=True
    )
    slot = slots(idr, earlier, experts)
    count = send_ref.shape[0]
    r = lax.broadcasted_iota(jnp.int32, (count, tok), 0)
    match = wanted_slot(r, count // 16) == slot
    part = quarter_of(r)
    span = width // 4
    for piece in range(0, span, 256):
        total = jnp.zeros((count, 256), F32)
        for q in range(4):
            chooser = jnp.where(jnp.logical_and(match, part == q), 1.0, 0.0).astype(BF)
            att = att_ref[:, q * span + piece : q * span + piece + 256].astype(F32)
            normed = (att * inverse).astype(BF)
            total = total + jnp.dot(chooser, normed, preferred_element_type=F32)
        send_ref[:, piece : piece + 256] = total.astype(BF)


def attend(kv, doc, q, ids, experts):
    tok, width = q.shape
    nctx = doc.shape[0]
    per = width // HD // (kv.shape[2] // HD)
    count = 16 * (experts // 2)
    vm = pl.BlockSpec(memory_space=pltpu.VMEM)
    return pl.pallas_call(
        functools.partial(attend_kernel, experts),
        out_shape=(
            jax.ShapeDtypeStruct((tok, width), BF),
            jax.ShapeDtypeStruct((count, width // 4), BF),
        ),
        in_specs=[vm, vm] + [pl.BlockSpec(memory_space=HBM)] * 2,
        out_specs=(vm, vm),
        scratch_shapes=[
            pltpu.VMEM((tok, width), BF),
            pltpu.VMEM((1, tok), jnp.int32),
            pltpu.VMEM((nctx // 2, per * tok, 2 * tok), F32),
            pltpu.VMEM((per * tok, HD), F32),
            pltpu.VMEM((per * tok, HD), F32),
            pltpu.VMEM((per * tok, HD), F32),
            pltpu.SemaphoreType.DMA((width // HD // per + 1,)),
        ],
        compiler_params=pltpu.CompilerParams(vmem_limit_bytes=48 << 20),
    )(kv, doc, q, ids)


def experts_kernel(
    nctx, nexp, send_ref, wgu_ref, wd_ref, early_ref, back_ref,
    came, rows, transit, hid0, hid1, made, ret, send2, back,
    a_sent, a_got, r_sent, r_got, t_sent, t_got, x_sent, x_got,
    h_sent, h_got, y_sent, y_got, d_sent, d_got, b_sent, b_got, wx, w_sent, w_got,
    wdx, wd_sent, wd_got, made_x, dx_sent,
):
    seg = nctx // 2
    half = seg // 2
    xy = nexp // 2
    span = send_ref.shape[1]
    width = 4 * span
    piece = xy
    units = wgu_ref.shape[0] // 2
    cols = wd_ref.shape[1]
    ctx = lax.axis_index("ctx")
    exp = lax.axis_index("exp")
    core = lax.rem(ctx, 2)
    pos = ctx // 2
    zhi = exp // xy
    place = lax.rem(exp, xy)
    layer = zhi * seg + pos
    layers = 2 * seg
    sibling = (ctx + 1 - 2 * core, exp)

    idle = jnp.logical_or(pos == 0, pos == seg - 1)
    near = jnp.logical_or(pos == 1, pos == seg - 2)
    beside = jnp.where(pos < half, ctx + 2, ctx - 2)
    outer = jnp.where(pos < half, ctx - 2, ctx + 2)
    parts = 2 * units // 16
    early = early_ref.shape[0] // 16
    ahead = early + min(parts // 3, parts - early)

    def weights(i, target):
        part = pl.ds(pl.multiple_of(i * 16, 16), 16)
        return remote(wgu_ref.at[part], wx.at[part], w_sent.at[i], w_got.at[i], (target, exp))

    def weights_down(i, target):
        n = 2 * units
        part = pl.ds(pl.multiple_of(i * n, n), n)
        return remote(wd_ref.at[part], wdx.at[part], wd_sent.at[i], wd_got.at[i], (target, exp))

    def at_layer(z, c):
        z = lax.rem(z + 2 * layers, layers)
        return (2 * lax.rem(z, seg) + c, (z // seg) * xy + place)

    def at_place(d):
        return (ctx, zhi * xy + d)

    barrier = pltpu.get_barrier_semaphore()

    @pl.loop(1, xy)
    def _(j):
        pl.semaphore_signal(
            barrier, inc=1, device_id=at_place(lax.rem(place + j, xy)), device_id_type=MESH
        )

    @pl.loop(1, 2 * layers)
    def _(j):
        me = 2 * layer + core
        n = lax.rem(me + j, 2 * layers)
        pl.semaphore_signal(
            barrier, inc=1, device_id=at_layer(n // 2, lax.rem(n, 2)), device_id_type=MESH
        )

    pl.semaphore_wait(barrier, xy - 1 + 2 * layers - 1)

    def block16(d):
        return pl.ds(pl.multiple_of(d * 16, 16), 16)

    def swap(src, dst, sent, got, d):
        out = remote(src.at[block16(d)], dst.at[block16(place)], sent.at[d], got.at[place], at_place(d))
        into = remote(src.at[block16(place)], dst.at[block16(d)], sent.at[place], got.at[d], at_place(d))
        return out, into

    def exchange(src, dst, sent, got):
        @pl.loop(1, xy)
        def _(j):
            swap(src, dst, sent, got, lax.rem(place + j, xy))[0].start()

        dst[block16(place)] = src[block16(place)]

    def exchange_wait(src, dst, sent, got):
        @pl.loop(1, xy)
        def _(j):
            swap(src, dst, sent, got, lax.rem(place + xy - j, xy))[1].wait_recv()

    def exchange_end(src, dst, sent, got):
        @pl.loop(1, xy)
        def _(j):
            swap(src, dst, sent, got, lax.rem(place + j, xy))[0].wait_send()

    @pl.when(idle)
    def _():
        for i in range(early, ahead):
            weights(i, beside).start()

    @pl.when(near)
    def _():
        wx[: 16 * early] = early_ref[...]

    exchange(send_ref, came, a_sent, a_got)
    exchange_wait(send_ref, came, a_sent, a_got)
    r = lax.broadcasted_iota(jnp.int32, (2 * xy, 16 * xy), 0)
    c = lax.broadcasted_iota(jnp.int32, (2 * xy, 16 * xy), 1)
    for side in range(2):
        z = zhi if side == 0 else 1 - zhi
        for q in range(4):
            pick = jnp.where(
                c == (r // 2) * 16 + q * 4 + 2 * z + lax.rem(r, 2), 1.0, 0.0
            ).astype(BF)
            got = jnp.dot(pick, came[...], preferred_element_type=F32).astype(BF)
            for h in range(2):
                kept = got[h * piece : (h + 1) * piece]
                if side == 0:
                    rows[layer, core, h, :, q * span : (q + 1) * span] = kept
                else:
                    transit[pos, h, :, q * span : (q + 1) * span] = kept

    def ring(z):
        return lax.rem(z + 2 * layers, layers)

    def rank_of(way):
        return pos if way == 1 else seg - 1 - pos

    def chunk_moves(way, t, h):
        d = 0 if way == 1 else 1
        k = rank_of(way)
        z = ring(layer - way * (t - 1))
        p = lax.rem(pos - way * (t - 1) + 2 * seg, seg)
        target = at_layer(layer + way, core)
        return [
            (
                jnp.logical_and(k < seg - 1, t <= k + 1 - half),
                remote(transit.at[p, h], transit.at[p, h], t_sent.at[d, t, h], t_got.at[p, h], target),
            ),
            (
                jnp.logical_and(k == seg - 1, t <= half),
                remote(transit.at[p, h], rows.at[z, core, h], t_sent.at[d, t, h], r_got.at[z, h], target),
            ),
            (
                jnp.logical_and(k < seg - 2, t <= k + 1 + half),
                remote(rows.at[z, core, h], rows.at[z, core, h], r_sent.at[d, t, h], r_got.at[z, h], target),
            ),
        ]

    def chunk_start(way, t, h):
        for cond, copy in chunk_moves(way, t, h):

            @pl.when(cond)
            def _():
                copy.start()

    def show(z, h, c):
        return remote(rows.at[z, c, h], rows.at[z, c, h], x_sent.at[z, h], x_got.at[z, h], sibling)

    for h in range(2):
        for way in (1, -1):
            chunk_start(way, 1, h)
        pl.when(jnp.logical_not(idle))(show(layer, h, core).start)

    steps = seg - 2 + half

    def rows_step(t):
        for j in range(2):
            i = ahead + 2 * (t - 1) + j

            @pl.when(jnp.logical_and(idle, i < parts))
            def _():
                weights(i, beside).start()

            n = 2 * (t - 1 - half) + j

            @pl.when(jnp.logical_and(idle, jnp.logical_and(n >= 0, n < seg)))
            def _():
                weights_down(n, beside).start()

        for h in range(2):
            for way in (1, -1):
                k = rank_of(way)
                z = ring(layer - way * t)
                p = lax.rem(pos - way * t + 2 * seg, seg)

                @pl.when(t <= k - half)
                def _():
                    remote(
                        transit.at[p, h], transit.at[p, h], t_sent.at[0, 0, h], t_got.at[p, h], sibling
                    ).wait_recv()

                needed = jnp.logical_and(k < seg - 1, t <= k + half)

                @pl.when(needed)
                def _():
                    remote(
                        rows.at[z, core, h], rows.at[z, core, h], r_sent.at[0, 0, h], r_got.at[z, h], sibling
                    ).wait_recv()

                chunk_start(way, t + 1, h)

                @pl.when(jnp.logical_and(needed, jnp.logical_not(idle)))
                def _():
                    show(z, h, core).start()

    mine, other = zhi, 1 - zhi
    quart = half // 2
    sizes = (seg, half, half)

    def layer_of(g, j):
        if g == 0:
            return mine * seg + j
        if g == 1:
            return other * seg + j + jnp.where(j >= quart, seg - half, 0)
        return other * seg + quart + j

    def ranges(g):
        if g == 0:
            return [(mine * seg, seg, 0)]
        if g == 1:
            return [(other * seg, quart, 0), (other * seg + seg - quart, quart, quart)]
        return [(other * seg + quart, half, 0)]

    def rows_shown(g):
        @pl.when(jnp.logical_not(idle))
        def _():
            @pl.loop(0, sizes[g])
            def _(j):
                for h in range(2):
                    show(layer_of(g, j), h, 1 - core).wait_recv()

    def hid(g, b):
        return hid0.at[b] if g == 0 else hid1.at[g - 1, b]

    def hid_move(g, b, sent, target):
        return remote(hid(g, b), hid(g, b), sent, h_got.at[g, b], target)

    def hid_came(g, b):
        hid_move(g, b, h_sent.at[0, 0, g], sibling).wait_recv()

    def hid_moves(way, t, g):
        d = 0 if way == 1 else 1
        k = rank_of(way)
        b = 2 * (pos - way * (t - 1)) + core
        return (
            jnp.logical_and(jnp.logical_and(k > 0, k < seg - 2), t <= k + 1),
            hid_move(g, b, h_sent.at[d, t, g], (ctx + 2 * way, exp)),
        )

    def hid_start(way, t, g):
        cond, copy = hid_moves(way, t, g)

        @pl.when(cond)
        def _():
            copy.start()

    def hid_show(g, b):
        return remote(hid(g, b), hid(g, b), y_sent.at[g, b], y_got.at[g, b], sibling)

    chunk = 4 * xy

    def units_of(w, g):
        x = [rows[pl.ds(z, n)].reshape(n * chunk, width) for z, n, _ in ranges(g)]
        x = x[0] if len(x) == 1 else jnp.concatenate(x, axis=0)
        both = lax.dot_general(w[...], x, NT, preferred_element_type=F32)
        gate, upper = both[:units], both[units:]
        return (gate / (1.0 + jnp.exp(-gate)) * upper).astype(BF)

    def gate_up(g):
        rows_shown(g)

        @pl.when(jnp.logical_not(idle))
        def _():
            hid(g, ctx)[...] = units_of(wgu_ref, g)
            for way in (1, -1):
                hid_start(way, 1, g)
            hid_show(g, ctx).start()

        @pl.when(near)
        def _():
            if g == 0:

                @pl.loop(early, parts)
                def _(i):
                    weights(i, outer).wait_recv()

            hid(g, outer)[...] = units_of(wx, g)
            for way in (1, -1):

                @pl.when(rank_of(way) == 1)
                def _():
                    hid_start(way, 2, g)

            hid_show(g, outer).start()

    def hid_step(g, t):
        for way in (1, -1):
            k = rank_of(way)
            b = 2 * (pos - way * t) + core

            @pl.when(jnp.logical_and(k < seg - 1, jnp.logical_and(t <= k, k + t > 2)))
            def _():
                hid_came(g, b)
                hid_start(way, t + 1, g)
                hid_show(g, b).start()

    fold = nctx // 4

    def slot_of(z, c):
        n = 2 * lax.rem(z, seg) + c
        return lax.rem(n, fold), z // seg, n // fold

    def home(source, sent, owner, z, c):
        n = zhi * nctx + owner
        slot = slot_of(zhi * seg + owner // 2, core)
        return remote(source.at[z, c], ret.at[slot], sent.at[2 * z + c], d_got.at[n], at_layer(z, c))

    def home_own(z, c):
        return home(made, d_sent, ctx, z, c)

    def home_outer(z, c):
        return home(made_x, dx_sent, outer, z, c)

    def home_from(z, c):
        n = (z // seg) * nctx + 2 * lax.rem(z, seg) + c
        return remote(
            made.at[z, c], ret.at[slot_of(z, c)], d_sent.at[2 * z + c], d_got.at[n], at_layer(z, c)
        )

    def send_home(g, w, into, move):
        hidden = (hid0[...] if g == 0 else hid1[g - 1]).reshape(nctx * units, sizes[g] * chunk)
        out = lax.dot_general(hidden, w[...], TN, preferred_element_type=F32)
        out = out.astype(BF).reshape(sizes[g], 2, 2 * xy, cols)
        for z, n, j in ranges(g):
            into[pl.ds(z, n)] = out[j : j + n]
        count = 2 * sizes[g]

        @pl.loop(0, count)
        def _(j):
            n = lax.rem(ctx + j, count)
            z, c = layer_of(g, n // 2), lax.rem(n, 2)

            @pl.when(jnp.logical_or(z != layer, c != core))
            def _():
                move(z, c).start()

    def down(g):
        @pl.when(jnp.logical_not(idle))
        def _():
            @pl.loop(0, seg)
            def _(p):
                hid_show(g, 2 * p + 1 - core).wait_recv()

            send_home(g, wd_ref, made, home_own)

        @pl.when(near)
        def _():
            if g == 0:

                @pl.loop(0, seg)
                def _(i):
                    weights_down(i, outer).wait_recv()

            send_home(g, wdx, made_x, home_outer)

    @pl.loop(1, seg - 1)
    def _(t):
        rows_step(t)

    gate_up(0)

    @pl.loop(1, quart + 1)
    def _(u):
        rows_step(seg - 2 + u)
        hid_step(0, u)

    gate_up(1)

    @pl.loop(quart + 1, half + 1)
    def _(u):
        rows_step(seg - 2 + u)
        hid_step(0, u)
        hid_step(1, u - quart)

    gate_up(2)

    @pl.loop(half + 1, seg - 1)
    def _(u):
        hid_step(0, u)
        hid_step(1, u - quart)
        hid_step(2, u - half)

    down(0)

    @pl.loop(seg - 1, seg - 1 + quart)
    def _(u):
        hid_step(1, u - quart)
        hid_step(2, u - half)

    down(1)

    @pl.loop(seg - 1 + quart, seg - 1 + half)
    def _(u):
        hid_step(2, u - half)

    down(2)

    exchange_end(send_ref, came, a_sent, a_got)

    @pl.loop(1, steps + 2)
    def _(t):
        for h in range(2):
            for way in (1, -1):
                for cond, copy in chunk_moves(way, t, h):

                    @pl.when(cond)
                    def _():
                        copy.wait_send()

    @pl.when(jnp.logical_not(idle))
    def _():
        @pl.loop(0, layers)
        def _(z):
            for h in range(2):
                show(z, h, core).wait_send()

    @pl.when(idle)
    def _():
        @pl.loop(early, parts)
        def _(i):
            weights(i, beside).wait_send()

        @pl.loop(0, seg)
        def _(i):
            weights_down(i, beside).wait_send()

    @pl.loop(1, seg + 1)
    def _(t):
        for g in range(3):
            for way in (1, -1):
                cond, copy = hid_moves(way, t, g)

                @pl.when(cond)
                def _():
                    copy.wait_send()

    @pl.when(jnp.logical_not(idle))
    def _():
        @pl.loop(0, seg)
        def _(p):
            for g in range(3):
                hid_show(g, 2 * p + core).wait_send()

    @pl.when(jnp.logical_not(idle))
    def _():
        ret[slot_of(layer, core)] = made[layer, core]

    @pl.when(near)
    def _():
        ret[slot_of(zhi * seg + outer // 2, core)] = made_x[layer, core]

    @pl.loop(0, 2 * layers)
    def _(n):
        z, c = n // 2, lax.rem(n, 2)
        p = z - zhi * seg
        local = jnp.logical_or(
            jnp.logical_and(jnp.logical_not(idle), p == pos),
            jnp.logical_and(near, p == outer // 2),
        )

        @pl.when(jnp.logical_not(jnp.logical_and(local, c == core)))
        def _():
            home_from(z, c).wait_recv()

    r = lax.broadcasted_iota(jnp.int32, (16 * xy, 16 * xy), 0)
    c = lax.broadcasted_iota(jnp.int32, (16 * xy, 16 * xy), 1)
    i = lax.rem(r, 4)
    place_back = jnp.where(
        c == ((i // 2) * 4 + quarter_of(r)) * 2 * xy + 2 * (r // 16) + lax.rem(i, 2), 1.0, 0.0
    ).astype(BF)
    for m in range(fold):
        got = ret[m].reshape(16 * xy, cols)
        send2[:, m * cols : (m + 1) * cols] = jnp.dot(
            place_back, got, preferred_element_type=F32
        ).astype(BF)
    exchange(send2, back, b_sent, b_got)

    @pl.when(jnp.logical_not(idle))
    def _():
        @pl.loop(1, 2 * layers)
        def _(j):
            n = lax.rem(2 * layer + core + j, 2 * layers)
            home_own(n // 2, lax.rem(n, 2)).wait_send()

    @pl.when(near)
    def _():
        @pl.loop(1, 2 * layers)
        def _(j):
            n = lax.rem(2 * layer + core + j, 2 * layers)
            home_outer(n // 2, lax.rem(n, 2)).wait_send()

    exchange_wait(send2, back, b_sent, b_got)
    back_ref[...] = back[...]
    exchange_end(send2, back, b_sent, b_got)


def run_experts(send, wgu, wd, wx, nctx, nexp):
    xy = nexp // 2
    seg = nctx // 2
    layers = 2 * seg
    span = send.shape[1]
    width = 4 * span
    units = wgu.shape[0] // 2
    cols = wd.shape[1]
    dma = pltpu.SemaphoreType.DMA
    vm = pl.BlockSpec(memory_space=pltpu.VMEM)
    return pl.pallas_call(
        functools.partial(experts_kernel, nctx, nexp),
        out_shape=jax.ShapeDtypeStruct(send.shape, BF),
        in_specs=[vm] * 4,
        out_specs=vm,
        scratch_shapes=[
            pltpu.VMEM(send.shape, BF),
            pltpu.VMEM((layers, 2, 2, xy, width), BF),
            pltpu.VMEM((seg, 2, xy, width), BF),
            pltpu.VMEM((nctx, units, seg * 4 * xy), BF),
            pltpu.VMEM((2, nctx, units, seg * 2 * xy), BF),
            pltpu.VMEM((layers, 2, 2 * xy, cols), BF),
            pltpu.VMEM((nctx // 4, 2, 4, 2 * xy, cols), BF),
            pltpu.VMEM(send.shape, BF),
            pltpu.VMEM(send.shape, BF),
            dma((xy,)),
            dma((xy,)),
            dma((2, layers, 2)),
            dma((layers, 2)),
            dma((2, layers, 2)),
            dma((seg, 2)),
            dma((layers, 2)),
            dma((layers, 2)),
            dma((2, layers, 3)),
            dma((3, nctx)),
            dma((3, nctx)),
            dma((3, nctx)),
            dma((2 * layers,)),
            dma((2 * layers,)),
            dma((xy,)),
            dma((xy,)),
            pltpu.VMEM(wgu.shape, BF),
            dma((2 * units // 16,)),
            dma((2 * units // 16,)),
            pltpu.VMEM(wd.shape, BF),
            dma((nctx // 2,)),
            dma((nctx // 2,)),
            pltpu.VMEM((layers, 2, 2 * xy, cols), BF),
            dma((2 * layers,)),
        ],
        compiler_params=pltpu.CompilerParams(
            collective_id=1, has_side_effects=True, vmem_limit_bytes=48 << 20
        ),
    )(send, wgu, wd, wx)


def join_kernel(experts, att_ref, back_ref, comb_hbm, id_hbm, out_ref, comb_ref, id_ref, got):
    loads = [
        pltpu.make_async_copy(comb_hbm, comb_ref, got.at[0]),
        pltpu.make_async_copy(id_hbm, id_ref, got.at[1]),
    ]
    for load in loads:
        load.start()
    for load in loads:
        load.wait()
    tok, width = att_ref.shape
    count, span = back_ref.shape
    idr = id_ref[...]
    idc = column(idr)
    before = lax.broadcasted_iota(jnp.int32, (tok, tok), 1) < lax.broadcasted_iota(
        jnp.int32, (tok, tok), 0
    )
    earlier = jnp.sum(
        jnp.where(jnp.logical_and(before, idc == idr), 1, 0), axis=1, keepdims=True
    )
    slot = slots(idc, earlier, experts)
    r = lax.broadcasted_iota(jnp.int32, (tok, count), 1)
    match = wanted_slot(r, count // 16) == slot
    part = quarter_of(r)
    comb = column(comb_ref[...])
    for q in range(4):
        chooser = jnp.where(jnp.logical_and(match, part == q), 1.0, 0.0).astype(BF)
        picked = jnp.dot(chooser, back_ref[...], preferred_element_type=F32)
        at = slice(q * span, (q + 1) * span)
        out_ref[:, at] = (att_ref[:, at].astype(F32) + comb * picked).astype(BF)


def join(att, back, comb, ids, experts):
    vm = pl.BlockSpec(memory_space=pltpu.VMEM)
    return pl.pallas_call(
        functools.partial(join_kernel, experts),
        out_shape=jax.ShapeDtypeStruct(att.shape, BF),
        in_specs=[vm, vm] + [pl.BlockSpec(memory_space=HBM)] * 2,
        out_specs=vm,
        scratch_shapes=[
            pltpu.VMEM(comb.shape, F32),
            pltpu.VMEM(ids.shape, jnp.int32),
            pltpu.SemaphoreType.DMA((2,)),
        ],
        compiler_params=pltpu.CompilerParams(vmem_limit_bytes=24 << 20),
    )(att, back, comb, ids)


def shards(query, keyval, doc_ids, route_ids, combine, w_gate_up, w_down):
    nctx = lax.axis_size("ctx")
    nexp = lax.axis_size("exp")
    units = w_gate_up.shape[2]
    wgu = w_gate_up[0].reshape(2 * units, -1)
    kv, doc, wx = spread(keyval[0], doc_ids, wgu, nctx)
    att, send = attend(kv, doc, query[0], route_ids, nexp)
    back = run_experts(send, wgu, w_down[0], wx, nctx, nexp)
    return join(att, back, combine, route_ids, nexp)[None]


def solution(mesh):
    placed = (
        P("exp", "ctx", None),
        P("exp", None, "ctx", None),
        P("exp", "ctx"),
        P("exp", "ctx"),
        P("exp", "ctx"),
        P("exp", None, "ctx", None),
        P("exp", None, "ctx"),
    )
    return jax.shard_map(
        shards, mesh=mesh, in_specs=placed, out_specs=P("exp", "ctx", None), check_vma=False
    )
```

```python
import functools

import jax
import jax.numpy as jnp
from jax import lax
from jax.experimental import pallas as pl
from jax.experimental.pallas import tpu as pltpu
from jax.sharding import PartitionSpec as P

HD = 128
CAP = 2
EPS = 1e-06
LOWEST = -1e30
LOG2E = 1.4426950408889634
REACH = 1024

BF = jnp.bfloat16
F32 = jnp.float32
MESH = pl.DeviceIdType.MESH
HBM = pltpu.HBM
NT = (((1,), (1,)), ((), ()))
TN = (((0,), (0,)), ((), ()))


def remote(src, dst, send_sem, recv_sem, target):
    return pltpu.make_async_remote_copy(
        src_ref=src,
        dst_ref=dst,
        send_sem=send_sem,
        recv_sem=recv_sem,
        device_id=target,
        device_id_type=MESH,
    )


def spread_kernel(
    nctx, kv_ref, doc_ref, w_ref, kv_out, doc_out, w_out,
    got, got_doc, sent, sent_doc, shown, shown_doc, kept, w_sent, w_got,
):
    tok = kv_ref.shape[1]
    seg = nctx // 2
    reach = min(seg - 1, -(-REACH // (2 * tok)))
    ctx = lax.axis_index("ctx")
    exp = lax.axis_index("exp")
    core = lax.rem(ctx, 2)
    pos = ctx // 2
    sibling = (ctx + 1 - 2 * core, exp)

    def block(b):
        return pl.ds(pl.multiple_of(b * tok, tok), tok)

    def neighbour(way):
        return (ctx + 2 * way, exp)

    def has(p):
        return jnp.logical_and(p >= 0, p < seg)

    barrier = pltpu.get_barrier_semaphore()
    pl.semaphore_signal(barrier, inc=1, device_id=sibling, device_id_type=MESH)
    for way in (1, -1):

        @pl.when(has(pos + way))
        def _():
            pl.semaphore_signal(barrier, inc=1, device_id=neighbour(way), device_id_type=MESH)

    pl.semaphore_wait(
        barrier, 1 + (pos > 0).astype(jnp.int32) + (pos < seg - 1).astype(jnp.int32)
    )

    def moves(b, sems, doc_sem, target, first):
        out = []
        for part in range(2):
            src = kv_ref.at[part] if first else kv_out.at[part, block(b)]
            out.append(
                remote(src, kv_out.at[part, block(b)], sems.at[part], got.at[b, part], target)
            )
        src = doc_ref.at[0:1] if first else doc_out.at[b]
        out.append(remote(src, doc_out.at[b], doc_sem, got_doc.at[b], target))
        return out

    def along(way, t, b):
        d = 0 if way == 1 else 1
        return moves(b, sent.at[d, t], sent_doc.at[d, t], neighbour(way), t == 0)

    def across(b, first):
        return moves(b, shown.at[b], shown_doc.at[b], sibling, first)

    for way in (1, -1):

        @pl.when(has(pos + way))
        def _():
            for copy in along(way, 0, ctx):
                copy.start()

    for copy in across(ctx, True):
        copy.start()
    idle = jnp.logical_or(pos == 0, pos == seg - 1)
    near = jnp.logical_or(pos == 1, pos == seg - 2)
    inwards = jnp.where(pos < seg // 2, ctx + 2, ctx - 2)
    early = w_out.shape[0] // 16

    def weights(i):
        part = pl.ds(i * 16, 16)
        return remote(w_ref.at[part], w_out.at[part], w_sent.at[i], w_got.at[i], (inwards, exp))

    @pl.when(idle)
    def _():
        for i in range(early):
            weights(i).start()

    own = [
        pltpu.make_async_copy(kv_ref, kv_out.at[:, block(ctx)], kept.at[0]),
        pltpu.make_async_copy(doc_ref, doc_out.at[ctx], kept.at[1]),
    ]
    for copy in own:
        copy.start()

    def finish(t):
        for way in (1, -1):
            source = pos - way * t
            b = 2 * source + core

            @pl.when(has(source))
            def _():
                if t > 0 or way == 1:
                    for copy in across(2 * source + 1 - core, False):
                        copy.wait_recv()
                    for copy in across(b, False):
                        copy.wait_send()
                if t < reach:

                    @pl.when(has(pos + way))
                    def _():
                        for copy in along(way, t, b):
                            copy.wait_send()

    for t in range(1, reach + 1):
        for way in (1, -1):
            source = pos - way * t
            b = 2 * source + core

            @pl.when(has(source))
            def _():
                there = across(b, False)
                on = along(way, t, b) if t < reach else None
                for n in range(3):
                    there[n].wait_recv()
                    if on is not None:

                        @pl.when(has(pos + way))
                        def _():
                            on[n].start()

                    there[n].start()

        if t >= 2:
            finish(t - 2)

    for copy in own:
        copy.wait()

    @pl.when(idle)
    def _():
        for i in range(early):
            weights(i).wait_send()

    @pl.when(near)
    def _():
        for i in range(early):
            weights(i).wait_recv()

    for t in range(max(0, reach - 1), reach + 1):
        finish(t)


def spread(kv, doc, wgu, nctx):
    early = max(1, wgu.shape[0] // 16 * 5 // 12)
    _, tok, width = kv.shape
    return pl.pallas_call(
        functools.partial(spread_kernel, nctx),
        out_shape=(
            jax.ShapeDtypeStruct((2, nctx * tok, width), BF),
            jax.ShapeDtypeStruct((nctx, 1, tok), jnp.int32),
            jax.ShapeDtypeStruct((16 * early, wgu.shape[1]), BF),
        ),
        in_specs=[pl.BlockSpec(memory_space=HBM)] * 3,
        out_specs=(pl.BlockSpec(memory_space=pltpu.VMEM),) * 3,
        scratch_shapes=[
            pltpu.SemaphoreType.DMA((nctx, 2)),
            pltpu.SemaphoreType.DMA((nctx,)),
            pltpu.SemaphoreType.DMA((2, 8, 2)),
            pltpu.SemaphoreType.DMA((2, 8)),
            pltpu.SemaphoreType.DMA((nctx, 2)),
            pltpu.SemaphoreType.DMA((nctx,)),
            pltpu.SemaphoreType.DMA((2,)),
            pltpu.SemaphoreType.DMA((early,)),
            pltpu.SemaphoreType.DMA((early,)),
        ],
        compiler_params=pltpu.CompilerParams(
            collective_id=0, has_side_effects=True, vmem_limit_bytes=16 << 20
        ),
    )(kv, doc, wgu)


def wanted_slot(r, columns):
    d, i = r // 16, lax.rem(r, 4)
    return (columns * (i // 2) + d) * CAP + lax.rem(i, 2)


def quarter_of(r):
    return lax.rem(r, 16) // 4


def column(row):
    n = row.shape[1]
    return jnp.transpose(jnp.broadcast_to(row, (n, n)))[:, :1]


def slots(ids, earlier, experts):
    kept = jnp.logical_and(ids < experts, earlier < CAP)
    return jnp.where(kept, ids * CAP + earlier, -1)


def attend_kernel(
    experts, kv_ref, doc_ref, q_hbm, id_hbm, att_ref, send_ref, q_ref, id_ref, s_scr, m_scr, l_scr, a_scr, q_got
):
    tok, width = q_ref.shape
    nctx = doc_ref.shape[0]
    share = width // (kv_ref.shape[2] // HD)
    loads = [
        pltpu.make_async_copy(
            q_hbm.at[:, g * share : (g + 1) * share],
            q_ref.at[:, g * share : (g + 1) * share],
            q_got.at[g],
        )
        for g in range(width // share)
    ]
    loads.append(pltpu.make_async_copy(id_hbm, id_ref, q_got.at[len(loads)]))
    for load in loads:
        load.start()
    groups = kv_ref.shape[2] // HD
    per = width // HD // groups
    step = 2 * tok
    seg = nctx // 2
    reach = min(seg - 1, -(-REACH // step))
    pos = lax.axis_index("ctx") // 2
    scale = HD ** (-0.5) * LOG2E

    where = lax.broadcasted_iota(jnp.int32, (nctx, 1, tok), 0) // 2
    docs = jnp.where(where < pos - reach, -1, jnp.where(where > pos + reach, 1 << 20, doc_ref[...]))
    qdoc = doc_ref[lax.axis_index("ctx")]
    part = tok // 2
    spans = []
    for p in range(2):
        low = jnp.min(qdoc[:, p * part : (p + 1) * part])
        high = jnp.max(qdoc[:, p * part : (p + 1) * part])
        begin = jnp.sum((docs < low).astype(jnp.int32))
        end = jnp.sum((docs <= high).astype(jnp.int32))
        spans.append((begin // step, (end + step - 1) // step))
    qdoc = column(qdoc)

    squares = jnp.zeros((tok, HD), F32)
    for g in range(groups):
        lanes = slice(g * HD, (g + 1) * HD)
        loads[g].wait()
        m_scr[...] = jnp.full(m_scr.shape, LOWEST, F32)
        l_scr[...] = jnp.zeros(l_scr.shape, F32)
        a_scr[...] = jnp.zeros(a_scr.shape, F32)

        for p in range(2):

            @pl.loop(*spans[p])
            def _(kb):
                keys = kv_ref[0, pl.ds(pl.multiple_of(kb * step, step), step), lanes]
                kdoc = jnp.concatenate([doc_ref[2 * kb, 0:1], doc_ref[2 * kb + 1, 0:1]], axis=1)
                bias = jnp.where(kdoc == qdoc[p * part : (p + 1) * part], 0.0, LOWEST).astype(F32)
                for h in range(per):
                    at = slice((g * per + h) * HD, (g * per + h + 1) * HD)
                    rows = slice(h * tok + p * part, h * tok + (p + 1) * part)
                    s = lax.dot_general(q_ref[p * part : (p + 1) * part, at], keys, NT, preferred_element_type=F32) + bias
                    s_scr[kb, rows] = s
                    m_scr[rows] = jnp.maximum(
                        m_scr[rows], jnp.maximum(s[:, :HD], s[:, HD:])
                    )

        for h in range(per):
            rows = slice(h * tok, (h + 1) * tok)
            m_scr[rows] = jnp.broadcast_to(
                jnp.max(m_scr[rows], axis=1, keepdims=True), (tok, HD)
            )

        for p in range(2):

            @pl.loop(*spans[p])
            def _(kb):
                values = kv_ref[1, pl.ds(pl.multiple_of(kb * step, step), step), lanes]
                for h in range(per):
                    rows = slice(h * tok + p * part, h * tok + (p + 1) * part)
                    top = m_scr[rows]
                    s = s_scr[kb, rows]
                    e = jnp.exp2((s - jnp.concatenate([top, top], axis=1)) * scale)
                    l_scr[rows] = l_scr[rows] + (e[:, :HD] + e[:, HD:])
                    a_scr[rows] = a_scr[rows] + jnp.dot(
                        e.astype(BF), values, preferred_element_type=F32
                    )

        for h in range(per):
            at = slice((g * per + h) * HD, (g * per + h + 1) * HD)
            rows = slice(h * tok, (h + 1) * tok)
            total = jnp.sum(l_scr[rows], axis=1, keepdims=True)
            mixed = (a_scr[rows] / total).astype(BF)
            att_ref[:, at] = mixed
            wide = mixed.astype(F32)
            squares = squares + wide * wide

    loads[-1].wait()
    inverse = lax.rsqrt(jnp.sum(squares, axis=1, keepdims=True) / width + EPS)
    idr = id_ref[...]
    idc = column(idr)
    before = lax.broadcasted_iota(jnp.int32, (tok, tok), 0) < lax.broadcasted_iota(
        jnp.int32, (tok, tok), 1
    )
    earlier = jnp.sum(
        jnp.where(jnp.logical_and(before, idc == idr), 1, 0), axis=0, keepdims=True
    )
    slot = slots(idr, earlier, experts)
    count = send_ref.shape[0]
    r = lax.broadcasted_iota(jnp.int32, (count, tok), 0)
    match = wanted_slot(r, count // 16) == slot
    part = quarter_of(r)
    span = width // 4
    for piece in range(0, span, 256):
        total = jnp.zeros((count, 256), F32)
        for q in range(4):
            chooser = jnp.where(jnp.logical_and(match, part == q), 1.0, 0.0).astype(BF)
            att = att_ref[:, q * span + piece : q * span + piece + 256].astype(F32)
            normed = (att * inverse).astype(BF)
            total = total + jnp.dot(chooser, normed, preferred_element_type=F32)
        send_ref[:, piece : piece + 256] = total.astype(BF)


def attend(kv, doc, q, ids, experts):
    tok, width = q.shape
    nctx = doc.shape[0]
    per = width // HD // (kv.shape[2] // HD)
    count = 16 * (experts // 2)
    vm = pl.BlockSpec(memory_space=pltpu.VMEM)
    return pl.pallas_call(
        functools.partial(attend_kernel, experts),
        out_shape=(
            jax.ShapeDtypeStruct((tok, width), BF),
            jax.ShapeDtypeStruct((count, width // 4), BF),
        ),
        in_specs=[vm, vm] + [pl.BlockSpec(memory_space=HBM)] * 2,
        out_specs=(vm, vm),
        scratch_shapes=[
            pltpu.VMEM((tok, width), BF),
            pltpu.VMEM((1, tok), jnp.int32),
            pltpu.VMEM((nctx // 2, per * tok, 2 * tok), F32),
            pltpu.VMEM((per * tok, HD), F32),
            pltpu.VMEM((per * tok, HD), F32),
            pltpu.VMEM((per * tok, HD), F32),
            pltpu.SemaphoreType.DMA((width // HD // per + 1,)),
        ],
        compiler_params=pltpu.CompilerParams(vmem_limit_bytes=48 << 20),
    )(kv, doc, q, ids)


def experts_kernel(
    nctx, nexp, send_ref, wgu_ref, wd_ref, early_ref, back_ref,
    came, rows, transit, hid0, hid1, made, ret, send2, back,
    a_sent, a_got, r_sent, r_got, t_sent, t_got, x_sent, x_got,
    h_sent, h_got, y_sent, y_got, d_sent, d_got, b_sent, b_got, wx, w_sent, w_got,
    wdx, wd_sent, wd_got, made_x, dx_sent,
):
    seg = nctx // 2
    half = seg // 2
    xy = nexp // 2
    span = send_ref.shape[1]
    width = 4 * span
    piece = xy
    units = wgu_ref.shape[0] // 2
    cols = wd_ref.shape[1]
    ctx = lax.axis_index("ctx")
    exp = lax.axis_index("exp")
    core = lax.rem(ctx, 2)
    pos = ctx // 2
    zhi = exp // xy
    place = lax.rem(exp, xy)
    layer = zhi * seg + pos
    layers = 2 * seg
    sibling = (ctx + 1 - 2 * core, exp)

    idle = jnp.logical_or(pos == 0, pos == seg - 1)
    near = jnp.logical_or(pos == 1, pos == seg - 2)
    beside = jnp.where(pos < half, ctx + 2, ctx - 2)
    outer = jnp.where(pos < half, ctx - 2, ctx + 2)
    parts = 2 * units // 16
    early = early_ref.shape[0] // 16
    ahead = early + min(parts // 3, parts - early)

    def weights(i, target):
        part = pl.ds(pl.multiple_of(i * 16, 16), 16)
        return remote(wgu_ref.at[part], wx.at[part], w_sent.at[i], w_got.at[i], (target, exp))

    def weights_down(i, target):
        n = 2 * units
        part = pl.ds(pl.multiple_of(i * n, n), n)
        return remote(wd_ref.at[part], wdx.at[part], wd_sent.at[i], wd_got.at[i], (target, exp))

    def at_layer(z, c):
        z = lax.rem(z + 2 * layers, layers)
        return (2 * lax.rem(z, seg) + c, (z // seg) * xy + place)

    def at_place(d):
        return (ctx, zhi * xy + d)

    barrier = pltpu.get_barrier_semaphore()

    @pl.loop(1, xy)
    def _(j):
        pl.semaphore_signal(
            barrier, inc=1, device_id=at_place(lax.rem(place + j, xy)), device_id_type=MESH
        )

    @pl.loop(1, 2 * layers)
    def _(j):
        me = 2 * layer + core
        n = lax.rem(me + j, 2 * layers)
        pl.semaphore_signal(
            barrier, inc=1, device_id=at_layer(n // 2, lax.rem(n, 2)), device_id_type=MESH
        )

    pl.semaphore_wait(barrier, xy - 1 + 2 * layers - 1)

    def block16(d):
        return pl.ds(pl.multiple_of(d * 16, 16), 16)

    def swap(src, dst, sent, got, d):
        out = remote(src.at[block16(d)], dst.at[block16(place)], sent.at[d], got.at[place], at_place(d))
        into = remote(src.at[block16(place)], dst.at[block16(d)], sent.at[place], got.at[d], at_place(d))
        return out, into

    def exchange(src, dst, sent, got):
        @pl.loop(1, xy)
        def _(j):
            swap(src, dst, sent, got, lax.rem(place + j, xy))[0].start()

        dst[block16(place)] = src[block16(place)]

    def exchange_wait(src, dst, sent, got):
        @pl.loop(1, xy)
        def _(j):
            swap(src, dst, sent, got, lax.rem(place + xy - j, xy))[1].wait_recv()

    def exchange_end(src, dst, sent, got):
        @pl.loop(1, xy)
        def _(j):
            swap(src, dst, sent, got, lax.rem(place + j, xy))[0].wait_send()

    @pl.when(idle)
    def _():
        for i in range(early, ahead):
            weights(i, beside).start()

    @pl.when(near)
    def _():
        wx[: 16 * early] = early_ref[...]

    exchange(send_ref, came, a_sent, a_got)
    exchange_wait(send_ref, came, a_sent, a_got)
    r = lax.broadcasted_iota(jnp.int32, (2 * xy, 16 * xy), 0)
    c = lax.broadcasted_iota(jnp.int32, (2 * xy, 16 * xy), 1)
    for side in range(2):
        z = zhi if side == 0 else 1 - zhi
        for q in range(4):
            pick = jnp.where(
                c == (r // 2) * 16 + q * 4 + 2 * z + lax.rem(r, 2), 1.0, 0.0
            ).astype(BF)
            got = jnp.dot(pick, came[...], preferred_element_type=F32).astype(BF)
            for h in range(2):
                kept = got[h * piece : (h + 1) * piece]
                if side == 0:
                    rows[layer, core, h, :, q * span : (q + 1) * span] = kept
                else:
                    transit[pos, h, :, q * span : (q + 1) * span] = kept

    def ring(z):
        return lax.rem(z + 2 * layers, layers)

    def rank_of(way):
        return pos if way == 1 else seg - 1 - pos

    def chunk_moves(way, t, h):
        d = 0 if way == 1 else 1
        k = rank_of(way)
        z = ring(layer - way * (t - 1))
        p = lax.rem(pos - way * (t - 1) + 2 * seg, seg)
        target = at_layer(layer + way, core)
        return [
            (
                jnp.logical_and(k < seg - 1, t <= k + 1 - half),
                remote(transit.at[p, h], transit.at[p, h], t_sent.at[d, t, h], t_got.at[p, h], target),
            ),
            (
                jnp.logical_and(k == seg - 1, t <= half),
                remote(transit.at[p, h], rows.at[z, core, h], t_sent.at[d, t, h], r_got.at[z, h], target),
            ),
            (
                jnp.logical_and(k < seg - 2, t <= k + 1 + half),
                remote(rows.at[z, core, h], rows.at[z, core, h], r_sent.at[d, t, h], r_got.at[z, h], target),
            ),
        ]

    def chunk_start(way, t, h):
        for cond, copy in chunk_moves(way, t, h):

            @pl.when(cond)
            def _():
                copy.start()

    def show(z, h, c):
        return remote(rows.at[z, c, h], rows.at[z, c, h], x_sent.at[z, h], x_got.at[z, h], sibling)

    for h in range(2):
        for way in (1, -1):
            chunk_start(way, 1, h)
        pl.when(jnp.logical_not(idle))(show(layer, h, core).start)

    steps = seg - 2 + half

    def rows_step(t):
        for j in range(2):
            i = ahead + 2 * (t - 1) + j

            @pl.when(jnp.logical_and(idle, i < parts))
            def _():
                weights(i, beside).start()

            n = 2 * (t - 1 - half) + j

            @pl.when(jnp.logical_and(idle, jnp.logical_and(n >= 0, n < seg)))
            def _():
                weights_down(n, beside).start()

        for h in range(2):
            for way in (1, -1):
                k = rank_of(way)
                z = ring(layer - way * t)
                p = lax.rem(pos - way * t + 2 * seg, seg)

                @pl.when(t <= k - half)
                def _():
                    remote(
                        transit.at[p, h], transit.at[p, h], t_sent.at[0, 0, h], t_got.at[p, h], sibling
                    ).wait_recv()

                needed = jnp.logical_and(k < seg - 1, t <= k + half)

                @pl.when(needed)
                def _():
                    remote(
                        rows.at[z, core, h], rows.at[z, core, h], r_sent.at[0, 0, h], r_got.at[z, h], sibling
                    ).wait_recv()

                chunk_start(way, t + 1, h)

                @pl.when(jnp.logical_and(needed, jnp.logical_not(idle)))
                def _():
                    show(z, h, core).start()

    mine, other = zhi, 1 - zhi
    quart = half // 2
    sizes = (seg, half, half)

    def layer_of(g, j):
        if g == 0:
            return mine * seg + j
        if g == 1:
            return other * seg + j + jnp.where(j >= quart, seg - half, 0)
        return other * seg + quart + j

    def ranges(g):
        if g == 0:
            return [(mine * seg, seg, 0)]
        if g == 1:
            return [(other * seg, quart, 0), (other * seg + seg - quart, quart, quart)]
        return [(other * seg + quart, half, 0)]

    def rows_shown(g):
        @pl.when(jnp.logical_not(idle))
        def _():
            @pl.loop(0, sizes[g])
            def _(j):
                for h in range(2):
                    show(layer_of(g, j), h, 1 - core).wait_recv()

    def hid(g, b):
        return hid0.at[b] if g == 0 else hid1.at[g - 1, b]

    def hid_move(g, b, sent, target):
        return remote(hid(g, b), hid(g, b), sent, h_got.at[g, b], target)

    def hid_came(g, b):
        hid_move(g, b, h_sent.at[0, 0, g], sibling).wait_recv()

    def hid_moves(way, t, g):
        d = 0 if way == 1 else 1
        k = rank_of(way)
        b = 2 * (pos - way * (t - 1)) + core
        return (
            jnp.logical_and(jnp.logical_and(k > 0, k < seg - 2), t <= k + 1),
            hid_move(g, b, h_sent.at[d, t, g], (ctx + 2 * way, exp)),
        )

    def hid_start(way, t, g):
        cond, copy = hid_moves(way, t, g)

        @pl.when(cond)
        def _():
            copy.start()

    def hid_show(g, b):
        return remote(hid(g, b), hid(g, b), y_sent.at[g, b], y_got.at[g, b], sibling)

    chunk = 4 * xy

    def units_of(w, g):
        x = [rows[pl.ds(z, n)].reshape(n * chunk, width) for z, n, _ in ranges(g)]
        x = x[0] if len(x) == 1 else jnp.concatenate(x, axis=0)
        both = lax.dot_general(w[...], x, NT, preferred_element_type=F32)
        gate, upper = both[:units], both[units:]
        return (gate / (1.0 + jnp.exp(-gate)) * upper).astype(BF)

    def gate_up(g):
        rows_shown(g)

        @pl.when(jnp.logical_not(idle))
        def _():
            hid(g, ctx)[...] = units_of(wgu_ref, g)
            for way in (1, -1):
                hid_start(way, 1, g)
            hid_show(g, ctx).start()

        @pl.when(near)
        def _():
            if g == 0:

                @pl.loop(early, parts)
                def _(i):
                    weights(i, outer).wait_recv()

            hid(g, outer)[...] = units_of(wx, g)
            for way in (1, -1):

                @pl.when(rank_of(way) == 1)
                def _():
                    hid_start(way, 2, g)

            hid_show(g, outer).start()

    def hid_step(g, t):
        for way in (1, -1):
            k = rank_of(way)
            b = 2 * (pos - way * t) + core

            @pl.when(jnp.logical_and(k < seg - 1, jnp.logical_and(t <= k, k + t > 2)))
            def _():
                hid_came(g, b)
                hid_start(way, t + 1, g)
                hid_show(g, b).start()

    fold = nctx // 4

    def slot_of(z, c):
        n = 2 * lax.rem(z, seg) + c
        return lax.rem(n, fold), z // seg, n // fold

    def home(source, sent, owner, z, c):
        n = zhi * nctx + owner
        slot = slot_of(zhi * seg + owner // 2, core)
        return remote(source.at[z, c], ret.at[slot], sent.at[2 * z + c], d_got.at[n], at_layer(z, c))

    def home_own(z, c):
        return home(made, d_sent, ctx, z, c)

    def home_outer(z, c):
        return home(made_x, dx_sent, outer, z, c)

    def home_from(z, c):
        n = (z // seg) * nctx + 2 * lax.rem(z, seg) + c
        return remote(
            made.at[z, c], ret.at[slot_of(z, c)], d_sent.at[2 * z + c], d_got.at[n], at_layer(z, c)
        )

    def send_home(g, w, into, move):
        hidden = (hid0[...] if g == 0 else hid1[g - 1]).reshape(nctx * units, sizes[g] * chunk)
        out = lax.dot_general(hidden, w[...], TN, preferred_element_type=F32)
        out = out.astype(BF).reshape(sizes[g], 2, 2 * xy, cols)
        for z, n, j in ranges(g):
            into[pl.ds(z, n)] = out[j : j + n]
        count = 2 * sizes[g]

        @pl.loop(0, count)
        def _(j):
            n = lax.rem(ctx + j, count)
            z, c = layer_of(g, n // 2), lax.rem(n, 2)

            @pl.when(jnp.logical_or(z != layer, c != core))
            def _():
                move(z, c).start()

    def down(g):
        @pl.when(jnp.logical_not(idle))
        def _():
            @pl.loop(0, seg)
            def _(p):
                hid_show(g, 2 * p + 1 - core).wait_recv()

            send_home(g, wd_ref, made, home_own)

        @pl.when(near)
        def _():
            if g == 0:

                @pl.loop(0, seg)
                def _(i):
                    weights_down(i, outer).wait_recv()

            send_home(g, wdx, made_x, home_outer)

    @pl.loop(1, seg - 1)
    def _(t):
        rows_step(t)

    gate_up(0)

    @pl.loop(1, quart + 1)
    def _(u):
        rows_step(seg - 2 + u)
        hid_step(0, u)

    gate_up(1)

    @pl.loop(quart + 1, half + 1)
    def _(u):
        rows_step(seg - 2 + u)
        hid_step(0, u)
        hid_step(1, u - quart)

    gate_up(2)

    @pl.loop(half + 1, seg - 1)
    def _(u):
        hid_step(0, u)
        hid_step(1, u - quart)
        hid_step(2, u - half)

    down(0)

    @pl.loop(seg - 1, seg - 1 + quart)
    def _(u):
        hid_step(1, u - quart)
        hid_step(2, u - half)

    down(1)

    @pl.loop(seg - 1 + quart, seg - 1 + half)
    def _(u):
        hid_step(2, u - half)

    down(2)

    exchange_end(send_ref, came, a_sent, a_got)

    @pl.loop(1, steps + 2)
    def _(t):
        for h in range(2):
            for way in (1, -1):
                for cond, copy in chunk_moves(way, t, h):

                    @pl.when(cond)
                    def _():
                        copy.wait_send()

    @pl.when(jnp.logical_not(idle))
    def _():
        @pl.loop(0, layers)
        def _(z):
            for h in range(2):
                show(z, h, core).wait_send()

    @pl.when(idle)
    def _():
        @pl.loop(early, parts)
        def _(i):
            weights(i, beside).wait_send()

        @pl.loop(0, seg)
        def _(i):
            weights_down(i, beside).wait_send()

    @pl.loop(1, seg + 1)
    def _(t):
        for g in range(3):
            for way in (1, -1):
                cond, copy = hid_moves(way, t, g)

                @pl.when(cond)
                def _():
                    copy.wait_send()

    @pl.when(jnp.logical_not(idle))
    def _():
        @pl.loop(0, seg)
        def _(p):
            for g in range(3):
                hid_show(g, 2 * p + core).wait_send()

    @pl.when(jnp.logical_not(idle))
    def _():
        ret[slot_of(layer, core)] = made[layer, core]

    @pl.when(near)
    def _():
        ret[slot_of(zhi * seg + outer // 2, core)] = made_x[layer, core]

    @pl.loop(0, 2 * layers)
    def _(n):
        z, c = n // 2, lax.rem(n, 2)
        p = z - zhi * seg
        local = jnp.logical_or(
            jnp.logical_and(jnp.logical_not(idle), p == pos),
            jnp.logical_and(near, p == outer // 2),
        )

        @pl.when(jnp.logical_not(jnp.logical_and(local, c == core)))
        def _():
            home_from(z, c).wait_recv()

    r = lax.broadcasted_iota(jnp.int32, (16 * xy, 16 * xy), 0)
    c = lax.broadcasted_iota(jnp.int32, (16 * xy, 16 * xy), 1)
    i = lax.rem(r, 4)
    place_back = jnp.where(
        c == ((i // 2) * 4 + quarter_of(r)) * 2 * xy + 2 * (r // 16) + lax.rem(i, 2), 1.0, 0.0
    ).astype(BF)
    for m in range(fold):
        got = ret[m].reshape(16 * xy, cols)
        send2[:, m * cols : (m + 1) * cols] = jnp.dot(
            place_back, got, preferred_element_type=F32
        ).astype(BF)
    exchange(send2, back, b_sent, b_got)

    @pl.when(jnp.logical_not(idle))
    def _():
        @pl.loop(1, 2 * layers)
        def _(j):
            n = lax.rem(2 * layer + core + j, 2 * layers)
            home_own(n // 2, lax.rem(n, 2)).wait_send()

    @pl.when(near)
    def _():
        @pl.loop(1, 2 * layers)
        def _(j):
            n = lax.rem(2 * layer + core + j, 2 * layers)
            home_outer(n // 2, lax.rem(n, 2)).wait_send()

    exchange_wait(send2, back, b_sent, b_got)
    back_ref[...] = back[...]
    exchange_end(send2, back, b_sent, b_got)


def run_experts(send, wgu, wd, wx, nctx, nexp):
    xy = nexp // 2
    seg = nctx // 2
    layers = 2 * seg
    span = send.shape[1]
    width = 4 * span
    units = wgu.shape[0] // 2
    cols = wd.shape[1]
    dma = pltpu.SemaphoreType.DMA
    vm = pl.BlockSpec(memory_space=pltpu.VMEM)
    return pl.pallas_call(
        functools.partial(experts_kernel, nctx, nexp),
        out_shape=jax.ShapeDtypeStruct(send.shape, BF),
        in_specs=[vm] * 4,
        out_specs=vm,
        scratch_shapes=[
            pltpu.VMEM(send.shape, BF),
            pltpu.VMEM((layers, 2, 2, xy, width), BF),
            pltpu.VMEM((seg, 2, xy, width), BF),
            pltpu.VMEM((nctx, units, seg * 4 * xy), BF),
            pltpu.VMEM((2, nctx, units, seg * 2 * xy), BF),
            pltpu.VMEM((layers, 2, 2 * xy, cols), BF),
            pltpu.VMEM((nctx // 4, 2, 4, 2 * xy, cols), BF),
            pltpu.VMEM(send.shape, BF),
            pltpu.VMEM(send.shape, BF),
            dma((xy,)),
            dma((xy,)),
            dma((2, layers, 2)),
            dma((layers, 2)),
            dma((2, layers, 2)),
            dma((seg, 2)),
            dma((layers, 2)),
            dma((layers, 2)),
            dma((2, layers, 3)),
            dma((3, nctx)),
            dma((3, nctx)),
            dma((3, nctx)),
            dma((2 * layers,)),
            dma((2 * layers,)),
            dma((xy,)),
            dma((xy,)),
            pltpu.VMEM(wgu.shape, BF),
            dma((2 * units // 16,)),
            dma((2 * units // 16,)),
            pltpu.VMEM(wd.shape, BF),
            dma((nctx // 2,)),
            dma((nctx // 2,)),
            pltpu.VMEM((layers, 2, 2 * xy, cols), BF),
            dma((2 * layers,)),
        ],
        compiler_params=pltpu.CompilerParams(
            collective_id=1, has_side_effects=True, vmem_limit_bytes=48 << 20
        ),
    )(send, wgu, wd, wx)


def join_kernel(experts, att_ref, back_ref, comb_hbm, id_hbm, out_ref, comb_ref, id_ref, got):
    loads = [
        pltpu.make_async_copy(comb_hbm, comb_ref, got.at[0]),
        pltpu.make_async_copy(id_hbm, id_ref, got.at[1]),
    ]
    for load in loads:
        load.start()
    for load in loads:
        load.wait()
    tok, width = att_ref.shape
    count, span = back_ref.shape
    idr = id_ref[...]
    idc = column(idr)
    before = lax.broadcasted_iota(jnp.int32, (tok, tok), 1) < lax.broadcasted_iota(
        jnp.int32, (tok, tok), 0
    )
    earlier = jnp.sum(
        jnp.where(jnp.logical_and(before, idc == idr), 1, 0), axis=1, keepdims=True
    )
    slot = slots(idc, earlier, experts)
    r = lax.broadcasted_iota(jnp.int32, (tok, count), 1)
    match = wanted_slot(r, count // 16) == slot
    part = quarter_of(r)
    comb = column(comb_ref[...])
    for q in range(4):
        chooser = jnp.where(jnp.logical_and(match, part == q), 1.0, 0.0).astype(BF)
        picked = jnp.dot(chooser, back_ref[...], preferred_element_type=F32)
        at = slice(q * span, (q + 1) * span)
        out_ref[:, at] = (att_ref[:, at].astype(F32) + comb * picked).astype(BF)


def join(att, back, comb, ids, experts):
    vm = pl.BlockSpec(memory_space=pltpu.VMEM)
    return pl.pallas_call(
        functools.partial(join_kernel, experts),
        out_shape=jax.ShapeDtypeStruct(att.shape, BF),
        in_specs=[vm, vm] + [pl.BlockSpec(memory_space=HBM)] * 2,
        out_specs=vm,
        scratch_shapes=[
            pltpu.VMEM(comb.shape, F32),
            pltpu.VMEM(ids.shape, jnp.int32),
            pltpu.SemaphoreType.DMA((2,)),
        ],
        compiler_params=pltpu.CompilerParams(vmem_limit_bytes=24 << 20),
    )(att, back, comb, ids)


def shards(query, keyval, doc_ids, route_ids, combine, w_gate_up, w_down):
    nctx = lax.axis_size("ctx")
    nexp = lax.axis_size("exp")
    units = w_gate_up.shape[2]
    wgu = w_gate_up[0].reshape(2 * units, -1)
    kv, doc, wx = spread(keyval[0], doc_ids, wgu, nctx)
    att, send = attend(kv, doc, query[0], route_ids, nexp)
    back = run_experts(send, wgu, w_down[0], wx, nctx, nexp)
    return join(att, back, combine, route_ids, nexp)[None]


def solution(mesh):
    placed = (
        P("exp", "ctx", None),
        P("exp", None, "ctx", None),
        P("exp", "ctx"),
        P("exp", "ctx"),
        P("exp", "ctx"),
        P("exp", None, "ctx", None),
        P("exp", None, "ctx"),
    )
    return jax.shard_map(
        shards, mesh=mesh, in_specs=placed, out_specs=P("exp", "ctx", None), check_vma=False
    )
```
